512 devices in a mesh: gx: 32 (over x, z_lo, core), gy: 16 (over z_hi, y).
Axes of the slice: x: 4, y: 4, z: 16 (z_hi: 4, z_lo: 4; z = z_hi * 4 + z_lo), core: 2. Of those that a mesh axis runs over, the one named last changes fastest.
Arguments:
- sky_image: float32 [4096, 4096], P('gx', 'gy'), may hold values from -6 to 6
- visibilities: bfloat16 [32, 16, 64, 2, 64], P('gx', 'gy'), may hold values from -6 to 6
- grid_kernels: bfloat16 [32, 16, 64, 64, 256], P('gx', 'gy'), may hold values from -0.75 to 0.75
- tile_counts: int32 [32, 16, 128], P('gx', 'gy'), may hold values from 0 to 16, as said below
- block_tiles: int32 [32, 16, 64], P('gx', 'gy'), may hold values from 0 to 127, as said below
- enter_weight: bfloat16 [3, 3, 32, 2], replicated, may hold values from -2 to 2
- enter_bias: float32 [32], replicated, may hold values from -3 to 3
- encode_weight: bfloat16 [3, 3, 32, 32], replicated, may hold values from -0.5 to 0.5
- encode_bias: float32 [32], replicated, may hold values from -3 to 3
- coarse_weight: bfloat16 [3, 3, 64, 32], replicated, may hold values from -0.5 to 0.5
- coarse_bias: float32 [64], replicated, may hold values from -3 to 3
- deeper_weight: bfloat16 [3, 3, 64, 64], replicated, may hold values from -0.375 to 0.375
- deeper_bias: float32 [64], replicated, may hold values from -3 to 3
- upward_weight: bfloat16 [32, 64], replicated, may hold values from -0.75 to 0.75
- skip_weight: bfloat16 [32, 32], replicated, may hold values from -1 to 1
- merge_bias: float32 [32], replicated, may hold values from -3 to 3
- decode_weight: bfloat16 [3, 3, 32, 32], replicated, may hold values from -0.5 to 0.5
- decode_bias: float32 [32], replicated, may hold values from -3 to 3
- output_weight: bfloat16 [3, 3, 1, 32], replicated, may hold values from -0.375 to 0.375
Outputs:
- dirty_image: float32 [4096, 4096], P('gx', 'gy')
- estimate: float32 [4096, 4096], P('gx', 'gy')
The draws below stay inside these ranges and needn't reach their ends.
Inputs may be any that keep to these rules, and one draw needn't show every extreme that they name: `tile_counts`: on each device the live blocks (the sum of its tile counts) number 1 to 64; the devices at the centre of the uv plane hold exactly 64, and the load falls away from the centre. No tile holds more than 16 blocks, and some tile of a centre device holds exactly that many. `block_tiles`: the first L slots of a device (L the sum of its tile counts) name their tiles in non-decreasing order, tile t as often as its count; the remaining slots hold 0 and carry no data.
All inputs are finite; a program needn't handle non-finite values.
Results may differ from the reference program's by a relative error of at most 0.015.
Values may be sent and summed in bfloat16 or wider, within the bound.
A program may use at most 128 MiB of HBM per device.

```python
import math
import jax
import jax.numpy as jnp
from jax import lax

ROWS_DEV = 128
COLS_DEV = 256
NR = 4096
NC = 4096
TILE_R = 8
TILE_C = 32
CELLS = 256
TILES_DEV = 128
VB = 64
BLK_DEV = 64
CH = 32
CH2 = 64
N_GX = 32
N_GY = 16


def plan_blocks(key):
    row_ids = jnp.arange(N_GX, dtype=jnp.int32)[:, None]
    col_ids = jnp.arange(N_GY, dtype=jnp.int32)[None, :]
    spread = jnp.abs(2 * row_ids + 1 - N_GX) + jnp.abs(2 * col_ids + 1 - N_GY) - 2
    baseline = BLK_DEV * 8 // (8 + spread)
    jitter = jax.random.randint(jax.random.fold_in(key, 11), (N_GX, N_GY), 0, 3)
    live_blocks = jnp.clip(baseline + jitter, 1, BLK_DEV).astype(jnp.int32)
    busy = jax.random.randint(jax.random.fold_in(key, 12), (N_GX, N_GY), 0, TILES_DEV).astype(jnp.int32)
    scores = jax.random.randint(jax.random.fold_in(key, 13), (N_GX, N_GY, TILES_DEV - 1), 0, 1 << 20)
    scores = scores * TILES_DEV + jnp.arange(TILES_DEV - 1, dtype=jnp.int32)[None, None, :]
    order = jnp.argsort(scores, axis=-1, stable=True).astype(jnp.int32)
    others = order + (order >= busy[:, :, None]).astype(jnp.int32)
    busy_count = jnp.minimum(live_blocks, BLK_DEV // 4)
    slots = jnp.arange(BLK_DEV, dtype=jnp.int32)[None, None, :]
    cycle = jnp.maximum(slots - busy_count[:, :, None], 0) % (TILES_DEV - 1)
    rest = jnp.take_along_axis(others, cycle.astype(jnp.int32), axis=-1)
    drawn_tiles = jnp.where(slots < busy_count[:, :, None], busy[:, :, None], rest)
    living = slots < live_blocks[:, :, None]
    ordered = jnp.sort(jnp.where(living, drawn_tiles, TILES_DEV), axis=-1)
    owners = jnp.where(living, ordered, 0).astype(jnp.int32)
    matches = (owners[..., None] == jnp.arange(TILES_DEV, dtype=jnp.int32)[None, None, None, :]) & living[..., None]
    counts = jnp.sum(matches.astype(jnp.int32), axis=2).astype(jnp.int32)
    return (counts, owners)


def draw_tile_counts(key, part):
    counts, owners = plan_blocks(key)
    return counts


def draw_block_tiles(key, part):
    counts, owners = plan_blocks(key)
    return owners


def levels(stream_key, shape, split, smallest, high):
    level = 1.0
    for position, parts in split:
        heights = jax.random.uniform(jax.random.fold_in(jax.random.fold_in(stream_key, 6), position), (parts,), jnp.float32, smallest / len(split), high / len(split))
        level = level * jnp.repeat(jnp.exp(heights), shape[position] // parts).reshape((-1,) + (1,) * (len(shape) - 1 - position))
    return level


def gaussian(own_key, shape, scale, reach, pieces=(), kind=jnp.bfloat16):
    entries = scale * jax.random.normal(own_key, shape, jnp.float32)
    if pieces:
        entries = entries * levels(own_key, shape, pieces, -0.22, 0.18)
    return jnp.clip(entries, -reach, reach).astype(kind)


def setup_inputs(seed: int = 0) -> dict:
    keys = jax.random.split(jax.random.key(seed), 20)
    return {
        "sky_image": gaussian(keys[0], (NR, NC), 1.0, 6.0, ((0, 32), (1, 16)), jnp.float32),
        "visibilities": gaussian(keys[1], (N_GX, N_GY, BLK_DEV, 2, VB), 1.0, 6.0, ((0, 32), (1, 16))),
        "grid_kernels": gaussian(keys[2], (N_GX, N_GY, BLK_DEV, VB, CELLS), VB ** -0.5, 0.75, ((0, 32), (1, 16))),
        "tile_counts": draw_tile_counts(jax.random.fold_in(keys[19], 71), 0),
        "block_tiles": draw_block_tiles(jax.random.fold_in(keys[19], 71), 0),
        "enter_weight": gaussian(keys[5], (3, 3, CH, 2), 9 ** -0.5, 2.0),
        "enter_bias": gaussian(keys[6], (CH,), 0.5, 3.0, (), jnp.float32),
        "encode_weight": gaussian(keys[7], (3, 3, CH, CH), (9 * CH // 2) ** -0.5, 0.5),
        "encode_bias": gaussian(keys[8], (CH,), 0.5, 3.0, (), jnp.float32),
        "coarse_weight": gaussian(keys[9], (3, 3, CH2, CH), (9 * CH // 2) ** -0.5, 0.5),
        "coarse_bias": gaussian(keys[10], (CH2,), 0.5, 3.0, (), jnp.float32),
        "deeper_weight": gaussian(keys[11], (3, 3, CH2, CH2), (9 * CH2 // 2) ** -0.5, 0.375),
        "deeper_bias": gaussian(keys[12], (CH2,), 0.5, 3.0, (), jnp.float32),
        "upward_weight": gaussian(keys[13], (CH, CH2), CH2 ** -0.5, 0.75),
        "skip_weight": gaussian(keys[14], (CH, CH), CH ** -0.5, 1.0),
        "merge_bias": gaussian(keys[15], (CH,), 0.5, 3.0, (), jnp.float32),
        "decode_weight": gaussian(keys[16], (3, 3, CH, CH), (9 * CH // 2) ** -0.5, 0.5),
        "decode_bias": gaussian(keys[17], (CH,), 0.5, 3.0, (), jnp.float32),
        "output_weight": gaussian(keys[18], (3, 3, 1, CH), (9 * CH) ** -0.5, 0.375),
    }


full_turn = 2.0 * math.pi

def tap_conv(window, weight, bias_vec):
    out_rows = window.shape[1] - 2
    out_cols = window.shape[2] - 2
    summed = None
    for row_shift in range(3):
        for col_shift in range(3):
            tap_term = jnp.einsum('oc,chw->ohw', weight[row_shift, col_shift], window[:, row_shift:row_shift + out_rows, col_shift:col_shift + out_cols], precision=lax.Precision.HIGHEST)
            summed = tap_term if summed is None else summed + tap_term
    return summed + bias_vec[:, None, None]

def conv_whole(values, weight, bias_vec, stripe, activate):
    line_total = values.shape[1]
    padded = jnp.pad(values, ((0, 0), (1, 1), (1, 1)))
    weight_wide = weight.astype(jnp.float32)

    def one_stripe(number):
        offset = (number * stripe).astype(jnp.int32)
        window = lax.dynamic_slice_in_dim(padded, offset, stripe + 2, 1).astype(jnp.float32)
        summed = tap_conv(window, weight_wide, bias_vec)
        if activate:
            return jax.nn.relu(summed).astype(jnp.bfloat16)
        return summed
    stacked = lax.map(one_stripe, jnp.arange(line_total // stripe, dtype=jnp.int32))
    return jnp.swapaxes(stacked, 0, 1).reshape(stacked.shape[1], line_total, values.shape[2])

def grid_row(inputs):
    visible, kernels, counts, owners = inputs
    contrib = jnp.einsum('jbkv,jbvc->jbkc', visible.astype(jnp.float32), kernels.astype(jnp.float32), precision=lax.Precision.HIGHEST)
    contrib = contrib.reshape(contrib.shape[0], contrib.shape[1], 2 * CELLS)
    live_blocks = lax.optimization_barrier(jnp.sum(counts, axis=-1))
    living = jnp.arange(BLK_DEV, dtype=jnp.int32)[None, :] < live_blocks[:, None]
    onehot = (owners[:, None, :] == jnp.arange(TILES_DEV, dtype=jnp.int32)[None, :, None]) & living[:, None, :]
    return jnp.einsum('jtb,jbx->jtx', onehot.astype(jnp.float32), contrib, precision=lax.Precision.HIGHEST)

def reference(sky_image, visibilities, grid_kernels, tile_counts, block_tiles, enter_weight, enter_bias, encode_weight, encode_bias, coarse_weight, coarse_bias, deeper_weight, deeper_bias, upward_weight, skip_weight, merge_bias, decode_weight, decode_bias, output_weight):
    tile_sums = lax.map(grid_row, (visibilities, grid_kernels, tile_counts, block_tiles))
    uv_grid = tile_sums.reshape(N_GX, N_GY, ROWS_DEV // TILE_R, COLS_DEV // TILE_C, 2, TILE_R, TILE_C)
    uv_grid = uv_grid.transpose(4, 0, 2, 5, 1, 3, 6).reshape(2, NR, NC)
    complex_grid = uv_grid[0] + 1j * uv_grid[1]
    raw_image = jnp.real(jnp.fft.ifft2(complex_grid)) * (NR * NC)
    row_sum = jnp.arange(NR, dtype=jnp.int32)[:, None] + jnp.arange(NC, dtype=jnp.int32)[None, :]
    parity = (1 - 2 * (row_sum % 2)).astype(jnp.float32)
    dirty_image = (raw_image * parity * (1.0 / math.sqrt(NR * NC))).astype(jnp.float32)
    net_input = jnp.stack([sky_image, dirty_image]).astype(jnp.bfloat16)
    entered = conv_whole(net_input, enter_weight, enter_bias, ROWS_DEV, True)
    encoded = conv_whole(entered, encode_weight, encode_bias, ROWS_DEV, True)
    pooled = encoded[:, 0::2, 0::2].astype(jnp.float32) + encoded[:, 1::2, 0::2].astype(jnp.float32) + encoded[:, 0::2, 1::2].astype(jnp.float32) + encoded[:, 1::2, 1::2].astype(jnp.float32)
    pooled = (pooled * 0.25).astype(jnp.bfloat16)
    coarse = conv_whole(pooled, coarse_weight, coarse_bias, ROWS_DEV // 2, True)
    deeper = conv_whole(coarse, deeper_weight, deeper_bias, ROWS_DEV // 2, True)
    upward_wide = upward_weight.astype(jnp.float32)
    skip_wide = skip_weight.astype(jnp.float32)

    def merge_stripe(number):
        coarse_start = (number * (ROWS_DEV // 2)).astype(jnp.int32)
        fine_start = (number * ROWS_DEV).astype(jnp.int32)
        low_part = lax.dynamic_slice_in_dim(deeper, coarse_start, ROWS_DEV // 2, 1).astype(jnp.float32)
        fine_part = lax.dynamic_slice_in_dim(encoded, fine_start, ROWS_DEV, 1).astype(jnp.float32)
        lifted = jnp.einsum('oc,chw->ohw', upward_wide, low_part, precision=lax.Precision.HIGHEST)
        lifted = jnp.repeat(jnp.repeat(lifted, 2, axis=1), 2, axis=2)
        joined = lifted + jnp.einsum('oc,chw->ohw', skip_wide, fine_part, precision=lax.Precision.HIGHEST)
        joined = joined + merge_bias[:, None, None]
        return jax.nn.relu(joined).astype(jnp.bfloat16)
    stacked = lax.map(merge_stripe, jnp.arange(NR // ROWS_DEV, dtype=jnp.int32))
    merged = jnp.swapaxes(stacked, 0, 1).reshape(CH, NR, NC)
    decoded = conv_whole(merged, decode_weight, decode_bias, ROWS_DEV, True)
    update = conv_whole(decoded, output_weight, jnp.zeros((1,), jnp.float32), ROWS_DEV, False)
    estimate = sky_image + update[0]
    return (dirty_image, estimate)
```

```python
import functools
import math

import jax
import jax.numpy as jnp
import numpy as np
from jax import lax
from jax.experimental import pallas as pl
from jax.experimental.pallas import tpu as pltpu
from jax.sharding import PartitionSpec as P

MESH = pl.DeviceIdType.MESH
F32 = jnp.float32
BF16 = jnp.bfloat16

NX, NY = 32, 16
SLABS = 18
STRIPES = 16
PIX = SLABS * STRIPES
PIX2 = PIX // 2
GROUPS = 18


def dot(a, b):
    return jnp.dot(a, b, preferred_element_type=F32)


def dot_nt(a, b):
    return lax.dot_general(a, b, (((1,), (1,)), ((), ())), preferred_element_type=F32)


def complex_block(c, s):
    return np.stack([np.stack([c, -s]), np.stack([s, c])])


def transform_constants():
    turn = 2.0 * math.pi
    y0 = np.arange(128)
    cells = np.arange(256)
    ang = turn * (np.outer(y0, y0) % 128) / 128
    first = complex_block(np.cos(ang), np.sin(ang))
    first = first.transpose(0, 2, 3, 1).reshape(256, 256)
    ang = turn * np.outer(y0, cells % 32) / 4096
    sign = np.where(y0 % 2 == 0, 1.0, -1.0)[:, None]
    twist1 = np.stack([np.cos(ang) * sign, np.sin(ang) * sign])
    short = np.arange(32)
    ang = turn * (np.outer(short, short) % 32) / 32
    c32, s32 = np.cos(ang), np.sin(ang)
    second = complex_block(c32, s32)
    second = np.einsum("abys,rt->yarbts", second, np.eye(8)).reshape(512, 512)
    third = complex_block(c32, s32)
    third = np.einsum("abxi,yz->ayxibz", third, np.eye(8)).reshape(512, 512)
    ang = turn * np.outer(y0, y0) / 4096
    twist2 = np.stack([np.cos(ang) * sign, np.sin(ang) * sign]) / 4096
    ang = turn * (np.outer(short, y0) % 32) / 32
    fourth = np.concatenate([np.cos(ang), -np.sin(ang)], axis=1)
    return (
        jnp.asarray(first, BF16),
        jnp.asarray(twist1, F32),
        jnp.asarray(second, BF16),
        jnp.asarray(third, BF16),
        jnp.asarray(twist2, F32),
        jnp.asarray(fourth, BF16),
        jnp.asarray(np.eye(128), BF16),
    )


def permutations():
    into = np.zeros((20, STRIPES, 384), np.float32)
    back = np.zeros((256, SLABS, STRIPES), np.float32)
    for w in range(-1, SLABS + 1):
        for s in range(STRIPES):
            col = SLABS * s + w - 8
            if 0 <= col < 264:
                into[w + 1, s, col] = 1
            elif -8 <= col < 0:
                into[w + 1, s, 384 + col] = 1
            if 0 <= col < 256 and 0 <= w < SLABS:
                back[col, w, s] = 1
    return jnp.asarray(into.reshape(320, 384), BF16), jnp.asarray(back.reshape(256, PIX), BF16)


def send_all(axis, count, me, source, landing, send_sem, recv_sem):
    def one(step, carry):
        other = lax.rem(me + step, count)
        pltpu.make_async_remote_copy(
            src_ref=source.at[other],
            dst_ref=landing.at[me],
            send_sem=send_sem,
            recv_sem=recv_sem,
            device_id={axis: other},
            device_id_type=MESH,
        ).start()
        return carry

    lax.fori_loop(1, count, one, 0)
    landing[me] = source[me]


def wait_bytes(ref, sem):
    pltpu.make_async_copy(ref, ref, sem).wait()


def grid_tiles(vis, owner, kernels):
    rows = lax.broadcasted_iota(jnp.int32, (256, 512), 0)
    tiles = rows // 2
    real = (rows % 2) == 0
    total = None
    for piece in range(8):
        lanes = slice(512 * piece, 512 * piece + 512)
        both = jnp.where(real, vis[0:1, lanes].astype(F32), vis[1:2, lanes].astype(F32))
        chosen = jnp.where(owner[0:1, lanes] == tiles, both, 0.0).astype(BF16)
        term = dot(chosen, kernels[lanes, :])
        total = term if total is None else total + term
    return total


def column_transform(held, first, twist1, second):
    turned = dot(first[...], held)
    real, imag = turned[:128], turned[128:]
    c, s = twist1[0], twist1[1]
    both = jnp.concatenate([real * c - imag * s, real * s + imag * c], axis=1).astype(BF16)
    return dot_nt(second[...], both)


def columns_up(held, eye):
    wide = held.astype(F32).reshape(16, 4, 8, 128)
    halves = []
    for y1 in range(2):
        parts = []
        for part in range(2):
            piece = wide[:, 2 * y1 + part].reshape(128, 128).astype(BF16)
            parts.append(dot_nt(eye, piece).reshape(16, 8, 128))
        halves.append(jnp.concatenate(parts, axis=1))
    return jnp.concatenate(halves, axis=0).astype(BF16)


def row_transform(held, third, twist2, fourth, store):
    turned = dot(third[...], held)
    for y in range(8):
        real = turned[32 * y : 32 * y + 32]
        imag = turned[256 + 32 * y : 256 + 32 * y + 32]
        real = jnp.concatenate([real] * 4, axis=0)
        imag = jnp.concatenate([imag] * 4, axis=0)
        c, s = twist2[0], twist2[1]
        both = jnp.concatenate([real * c - imag * s, real * s + imag * c], axis=1).astype(BF16)
        store(y, dot_nt(fourth[...], both))


def exchange_kernel(
    vis,
    owner,
    kernels,
    sky,
    first,
    twist1,
    second,
    third,
    twist2,
    fourth,
    eye,
    dirty_out,
    rows_out,
    cols_out,
    tiles,
    landed1,
    bands,
    landed2,
    ups,
    landed3,
    image,
    downs,
    landed4,
    sides,
    sky_rows,
    sky_sides,
    sky_cols,
    sky_own,
    send_sem,
    recv_sem,
):
    gx, gy = lax.axis_index("gx"), lax.axis_index("gy")
    barrier = pltpu.get_barrier_semaphore()

    def greet(axis, count, me):
        def one(step, carry):
            pl.semaphore_signal(
                barrier, inc=1, device_id={axis: lax.rem(me + step, count)}, device_id_type=MESH
            )
            return carry

        lax.fori_loop(1, count, one, 0)

    greet("gy", NY, gy)
    greet("gx", NX, gx)

    sky_own[...] = sky[...].astype(BF16)
    summed = grid_tiles(vis, owner, kernels)
    tiles[...] = summed.astype(BF16).reshape(16, 16, 256)
    pl.semaphore_wait(barrier, NX + NY - 2)

    send_all("gy", NY, gy, tiles, landed1, send_sem.at[0], recv_sem.at[0])

    def to_side(source, target, slot, axis, other):
        return pltpu.make_async_remote_copy(
            src_ref=source,
            dst_ref=target,
            send_sem=send_sem.at[slot],
            recv_sem=recv_sem.at[slot],
            device_id={axis: other},
            device_id_type=MESH,
        )

    down_x, up_x = lax.rem(gx + 1, NX), lax.rem(gx + NX - 1, NX)
    right_y, left_y = lax.rem(gy + 1, NY), lax.rem(gy + NY - 1, NY)
    row_copies = [
        to_side(sky_own.at[pl.ds(112, 16)], sky_rows.at[0], 4, "gx", down_x),
        to_side(sky_own.at[pl.ds(0, 16)], sky_rows.at[1], 5, "gx", up_x),
    ]
    for copy in row_copies:
        copy.start()

    wait_bytes(landed1.at[pl.ds(0, 15)], recv_sem.at[0])
    turned = column_transform(landed1[...].reshape(256, 256), first, twist1, second)
    bands[...] = turned.astype(BF16).reshape(16, 32, 128)
    send_all("gy", NY, gy, bands, landed2, send_sem.at[1], recv_sem.at[1])

    for copy in row_copies:
        copy.wait()
    for half in range(2):
        lanes = slice(128 * half, 128 * half + 128)
        sky_cols[half, 0:16] = sky_rows[0, :, lanes]
        sky_cols[half, 16:144] = sky_own[:, lanes]
        sky_cols[half, 144:160] = sky_rows[1, :, lanes]
    col_copies = [
        to_side(sky_cols.at[1], sky_sides.at[0], 6, "gy", right_y),
        to_side(sky_cols.at[0], sky_sides.at[1], 7, "gy", left_y),
    ]
    for copy in col_copies:
        copy.start()

    wait_bytes(landed2.at[pl.ds(0, 15)], recv_sem.at[1])
    ups[...] = columns_up(landed2[...], eye[...])
    send_all("gx", NX, gx, ups, landed3, send_sem.at[2], recv_sem.at[2])

    wait_bytes(landed3.at[pl.ds(0, 31)], recv_sem.at[2])

    def store(y, value):
        image[pl.ds(8 + y, 32, stride=8), :] = value

    image[0:8] = jnp.zeros((8, 128), F32)
    image[264:272] = jnp.zeros((8, 128), F32)
    row_transform(landed3[...].reshape(512, 128), third, twist2, fourth, store)
    whole = image[...].reshape(34, 8, 128)
    lane = lax.broadcasted_iota(jnp.int32, (32, 8, 128), 2)
    outer = jnp.where(lane < 64, whole[2:34], whole[0:32])
    downs[...] = jnp.concatenate([whole[1:33], outer], axis=1).astype(BF16)
    send_all("gx", NX, gx, downs, landed4, send_sem.at[3], recv_sem.at[3])

    for copy in col_copies:
        copy.wait()
    rows_out[...] = sky_rows[...]
    cols_out[...] = sky_sides[...]

    wait_bytes(landed4.at[pl.ds(0, 31)], recv_sem.at[3])
    side_copies = [
        to_side(landed4.at[31], sides.at[0], 8, "gy", right_y),
        to_side(landed4.at[0], sides.at[1], 9, "gy", left_y),
    ]
    for copy in side_copies:
        copy.start()
    dirty_out[0:32] = landed4[...]
    for copy in side_copies:
        copy.wait()
    dirty_out[32:34] = sides[...]
    wait_bytes(tiles.at[pl.ds(0, 15)], send_sem.at[0])
    wait_bytes(bands.at[pl.ds(0, 15)], send_sem.at[1])
    wait_bytes(ups.at[pl.ds(0, 31)], send_sem.at[2])
    wait_bytes(downs.at[pl.ds(0, 31)], send_sem.at[3])


def exchange(vis, owner, kernels, sky):
    vmem = pl.BlockSpec(memory_space=pltpu.VMEM)
    constants = transform_constants()
    return pl.pallas_call(
        exchange_kernel,
        out_shape=(
            jax.ShapeDtypeStruct((34, 16, 128), BF16),
            jax.ShapeDtypeStruct((2, 16, 256), BF16),
            jax.ShapeDtypeStruct((2, 160, 128), BF16),
        ),
        in_specs=[vmem] * 11,
        out_specs=(vmem, vmem, vmem),
        scratch_shapes=[
            pltpu.VMEM((16, 16, 256), BF16),
            pltpu.VMEM((16, 16, 256), BF16),
            pltpu.VMEM((16, 32, 128), BF16),
            pltpu.VMEM((16, 32, 128), BF16),
            pltpu.VMEM((32, 16, 128), BF16),
            pltpu.VMEM((32, 16, 128), BF16),
            pltpu.VMEM((272, 128), F32),
            pltpu.VMEM((32, 16, 128), BF16),
            pltpu.VMEM((32, 16, 128), BF16),
            pltpu.VMEM((2, 16, 128), BF16),
            pltpu.VMEM((2, 16, 256), BF16),
            pltpu.VMEM((2, 160, 128), BF16),
            pltpu.VMEM((2, 160, 128), BF16),
            pltpu.VMEM((128, 256), BF16),
            pltpu.SemaphoreType.DMA((10,)),
            pltpu.SemaphoreType.DMA((10,)),
        ],
        compiler_params=pltpu.CompilerParams(
            collective_id=0, has_side_effects=True, vmem_limit_bytes=40 << 20
        ),
        name="exchange",
    )(vis, owner, kernels, sky, *constants)


def band(dst, tiles, taps_high, rows, start, lane_id, count, per_dc):
    for dc in range(3):
        for row in range(rows):
            block = None
            for p in range(3):
                out_row = row - start - p
                if 0 <= out_row < count:
                    term = jnp.where(lane_id == out_row, tiles[3 * p + dc].astype(F32), 0.0)
                    block = term if block is None else block + term
            if block is None:
                block = jnp.zeros(lane_id.shape, F32)
            at = dc * per_dc + row * taps_high
            dst[at : at + taps_high, :] = block.astype(BF16)


def network_kernel(
    sky,
    dirty_in,
    rows_in,
    cols_in,
    into,
    back,
    eye,
    biases,
    enter_t,
    encode_t,
    coarse_t,
    deeper_t,
    decode_t,
    output_t,
    upward_t,
    skip_t,
    dirty_out,
    estimate_out,
    window,
    entry,
    fine_a,
    fine_b,
    fine_c,
    pooled,
    coarse,
    deep,
    mask,
    w_enter,
    w_encode,
    w_coarse,
    w_deeper,
    w_decode,
    w_output,
    w_upward,
    w_skip,
    w_pool,
    drawn,
):
    gx, gy = lax.axis_index("gx"), lax.axis_index("gy")
    last_x, last_y = lax.axis_size("gx") - 1, lax.axis_size("gy") - 1
    keep_top = jnp.where(gx == 0, 0.0, 1.0).astype(F32)
    keep_bottom = jnp.where(gx == last_x, 0.0, 1.0).astype(F32)

    lane32 = lax.broadcasted_iota(jnp.int32, (32, 256), 1)
    band(w_encode, encode_t, 32, 16, 3, lane32 // 32, 8, 512)
    band(w_decode, decode_t, 32, 16, 3, lane32 // 32, 8, 512)
    band(w_coarse, coarse_t, 32, 12, 3, lane32 // 64, 4, 384)
    lane64 = lax.broadcasted_iota(jnp.int32, (64, 256), 1)
    band(w_deeper, deeper_t, 64, 8, 1, lane64 // 64, 4, 512)
    lane_out = lax.broadcasted_iota(jnp.int32, (32, 128), 1)
    band(w_output, output_t, 32, 16, 3, lane_out % 8, 8, 512)
    for row in range(4):
        term = jnp.where(lane64 // 64 == row, upward_t[...].astype(F32), 0.0)
        w_upward[64 * row : 64 * row + 64, :] = term.astype(BF16)
    for row in range(8):
        term = jnp.where(lane32 // 32 == row, skip_t[...].astype(F32), 0.0)
        w_skip[32 * row : 32 * row + 32, :] = term.astype(BF16)
    rows512 = lax.broadcasted_iota(jnp.int32, (512, 128), 0)
    lanes512 = lax.broadcasted_iota(jnp.int32, (512, 128), 1)
    pairs = ((rows512 % 256) // 64 == lanes512 // 32) & (rows512 % 32 == lanes512 % 32)
    w_pool[...] = jnp.where(pairs, 0.25, 0.0).astype(BF16)
    row_id = lax.broadcasted_iota(jnp.int32, (64, 256), 0)
    for variant in range(4):
        for dc in range(3):
            for channel in range(2):
                block = jnp.zeros((64, 256), F32)
                for p in range(3):
                    tap = 6 * p + 2 * dc + channel
                    hit = row_id - 15 - 8 * variant - p == lane64 // 32
                    block = block + jnp.where(hit, enter_t[tap : tap + 1, :].astype(F32), 0.0)
                at = dc * 128 + channel * 64
                w_enter[variant, at : at + 64, :] = block.astype(BF16)

    slab = lax.broadcasted_iota(jnp.int32, (20, 16, 128), 0)
    stripe = lax.broadcasted_iota(jnp.int32, (20, 16, 128), 1)
    col = SLABS * stripe + slab - 9 + 256 * gy
    mask[...] = jnp.where((col >= 0) & (col < 256 * (last_y + 1)), 1.0, 0.0).astype(F32)

    lane = lax.broadcasted_iota(jnp.int32, (160, 128), 1)
    beside = jnp.where(lane < 64, cols_in[1].astype(F32), cols_in[0].astype(F32))
    above = rows_in[0].astype(F32)[8:16] * keep_top
    below = rows_in[1].astype(F32)[0:8] * keep_bottom
    zeros = jnp.zeros((32, 256), F32)
    window[0, :, 0:256] = jnp.concatenate(
        [zeros[:16], above, sky[...], below, zeros], axis=0
    ).astype(BF16)
    beside = jnp.concatenate(
        [
            zeros[:16, :128],
            beside[8:16] * keep_top,
            beside[16:144],
            beside[144:152] * keep_bottom,
            zeros[:, :128],
        ],
        axis=0,
    )
    window[0, :, 256:384] = beside.astype(BF16)
    wide = dirty_in[...].astype(F32)
    gap = jnp.zeros((112, 128), F32)
    parts = []
    for half in range(2):
        rows8 = slice(8 * half, 8 * half + 8)
        stacked = jnp.concatenate(
            [wide[0:32, rows8].reshape(256, 128), wide[33, rows8], gap, wide[32, rows8]], axis=0
        )
        parts.append(dot_nt(eye[...], stacked.astype(BF16)))
    dirty_out[...] = parts[0][:, 0:256]
    zeros = jnp.zeros((32, 384), F32)
    window[1] = jnp.concatenate(
        [zeros[:16], parts[1][120:128] * keep_top, parts[0], parts[1][0:8] * keep_bottom, zeros],
        axis=0,
    ).astype(BF16)
    for q in range(5):
        rows64 = slice(32 * q, 32 * q + 64)
        both = jnp.concatenate([window[0, rows64], window[1, rows64]], axis=0)
        placed = dot_nt(into[...], both).reshape(20, 16, 128) * mask[...]
        entry[q] = placed.astype(BF16)

    blank = jnp.zeros((20, 16, 128), BF16)
    for ref, top in ((fine_a, 37), (fine_b, 37), (fine_c, 37), (pooled, 19), (coarse, 37)):
        ref[0] = blank[: ref.shape[1]]
        ref[top] = blank[: ref.shape[1]]

    def row_keep(group):
        top = jnp.where(group == 0, keep_top, 1.0)
        bottom = jnp.where(group == GROUPS - 1, keep_bottom, 1.0)
        return top * bottom

    def put(ref, at, value, slabs):
        ref[at, 1 : slabs + 1] = value.astype(BF16)
        ref[at, 0] = pltpu.roll(value[slabs - 1], 1, 0).astype(BF16)
        ref[at, slabs + 1] = pltpu.roll(value[0], STRIPES - 1, 0).astype(BF16)

    def finish(total, bias_row, keep):
        value = jnp.maximum(total + biases[bias_row : bias_row + 1, :], 0.0)
        scaled = mask[1:19] * keep
        return [
            value[:, 128 * h : 128 * h + 128].reshape(SLABS, 16, 128) * scaled for h in range(2)
        ]

    def gathered(ref, at, high, slabs):
        pieces = [
            ref[at + h, dc : dc + slabs].reshape(slabs * 16, 128)
            for dc in range(3)
            for h in range(high)
        ]
        return jnp.concatenate(pieces, axis=1)

    def enter_step(group, carry):
        tile, variant = group // 4, group % 4
        pieces = [entry[tile, dc : dc + SLABS].reshape(PIX, 128) for dc in range(3)]
        total = dot(jnp.concatenate(pieces, axis=1), w_enter[variant])
        for h, value in enumerate(finish(total, 0, row_keep(group))):
            put(fine_a, 2 * group + 1 + h, value, SLABS)
        return carry

    lax.fori_loop(0, GROUPS, enter_step, 0)

    def encode_step(group, carry):
        total = dot(gathered(fine_a, 2 * group, 4, SLABS), w_encode[...])
        halves = finish(total, 1, row_keep(group))
        evens, odds = [], []
        for h, value in enumerate(halves):
            put(fine_b, 2 * group + 1 + h, value, SLABS)
            split = value.reshape(SLABS // 2, 2, 16, 128)
            evens.append(split[:, 0].reshape(PIX2, 128))
            odds.append(split[:, 1].reshape(PIX2, 128))
        small = dot(jnp.concatenate(evens + odds, axis=1).astype(BF16), w_pool[...])
        put(pooled, group + 1, small.reshape(SLABS // 2, 16, 128), SLABS // 2)
        return carry

    lax.fori_loop(0, GROUPS, encode_step, 0)

    def coarse_mask(keep):
        even = mask[1:19].reshape(SLABS // 2, 2, 16, 128)[:, 0]
        return even * keep

    def coarse_step(group, carry):
        total = dot(gathered(pooled, group, 3, SLABS // 2), w_coarse[...])
        value = jnp.maximum(total + biases[2:3, :], 0.0)
        scaled = coarse_mask(row_keep(group))
        for h in range(2):
            half = value[:, 128 * h : 128 * h + 128].reshape(SLABS // 2, 16, 128) * scaled
            put(coarse, 2 * group + 1 + h, half, SLABS // 2)
        return carry

    lax.fori_loop(0, GROUPS, coarse_step, 0)

    def merge_step(group, carry):
        total = dot(gathered(coarse, 2 * group, 4, SLABS // 2), w_deeper[...])
        value = jnp.maximum(total + biases[3:4, :], 0.0).astype(BF16)
        lifted = dot(value, w_upward[...]).reshape(SLABS // 2, 1, 16, 256)
        own = jnp.concatenate(
            [fine_b[2 * group + 1 + h, 1:19].reshape(PIX, 128) for h in range(2)], axis=1
        )
        skipped = dot(own, w_skip[...]).reshape(SLABS // 2, 2, 16, 256)
        total = (skipped + lifted).reshape(PIX, 256)
        for h, half in enumerate(finish(total, 4, row_keep(group))):
            put(fine_a, 2 * group + 1 + h, half, SLABS)
        return carry

    lax.fori_loop(0, GROUPS, merge_step, 0)

    def decode_step(group, carry):
        total = dot(gathered(fine_a, 2 * group, 4, SLABS), w_decode[...])
        for h, half in enumerate(finish(total, 5, row_keep(group))):
            put(fine_c, 2 * group + 1 + h, half, SLABS)
        return carry

    lax.fori_loop(0, GROUPS, decode_step, 0)

    lane_row = lax.broadcasted_iota(jnp.int32, (PIX, 128), 1) // 8

    def output_step(group, carry):
        total = dot(gathered(fine_c, 2 * group, 4, SLABS), w_output[...])
        drawn[...] = jnp.where(lane_row == group - 1, total, drawn[...])
        return carry

    drawn[...] = jnp.zeros((PIX, 128), F32)
    lax.fori_loop(1, GROUPS - 1, output_step, 0)

    update = drawn[...]
    high = update.astype(BF16)
    low = (update - high.astype(F32)).astype(BF16)
    ordered = dot(back[...], high) + dot(back[...], low)
    estimate_out[...] = sky[...] + ordered.T


def network(sky, dirty_in, rows_in, cols_in, weights):
    vmem = pl.BlockSpec(memory_space=pltpu.VMEM)
    into, back = permutations()
    eye = jnp.asarray(np.eye(128), BF16)
    operands = (sky, dirty_in, rows_in, cols_in, into, back, eye) + weights
    return pl.pallas_call(
        network_kernel,
        out_shape=(
            jax.ShapeDtypeStruct((128, 256), F32),
            jax.ShapeDtypeStruct((128, 256), F32),
        ),
        in_specs=[vmem] * len(operands),
        out_specs=(vmem, vmem),
        scratch_shapes=[
            pltpu.VMEM((2, 192, 384), BF16),
            pltpu.VMEM((5, 20, 16, 128), BF16),
            pltpu.VMEM((38, 20, 16, 128), BF16),
            pltpu.VMEM((38, 20, 16, 128), BF16),
            pltpu.VMEM((38, 20, 16, 128), BF16),
            pltpu.VMEM((20, 11, 16, 128), BF16),
            pltpu.VMEM((38, 11, 16, 128), BF16),
            pltpu.VMEM((8, 128), BF16),
            pltpu.VMEM((20, 16, 128), F32),
            pltpu.VMEM((4, 384, 256), BF16),
            pltpu.VMEM((1536, 256), BF16),
            pltpu.VMEM((1152, 256), BF16),
            pltpu.VMEM((1536, 256), BF16),
            pltpu.VMEM((1536, 256), BF16),
            pltpu.VMEM((1536, 128), BF16),
            pltpu.VMEM((256, 256), BF16),
            pltpu.VMEM((256, 256), BF16),
            pltpu.VMEM((512, 128), BF16),
            pltpu.VMEM((PIX, 128), F32),
        ],
        compiler_params=pltpu.CompilerParams(vmem_limit_bytes=48 << 20),
        name="network",
    )(*operands)


def tap_tiles(weight, copies):
    turned = jnp.swapaxes(weight, 2, 3)
    turned = jnp.tile(turned, (1, 1, 1, copies))
    return turned.reshape(9, turned.shape[2], turned.shape[3])


def network_weights(ew, eb, nw, nb, cw, cb, dw, db, uw, sw, mb, ow, ob, fw):
    biases = jnp.stack(
        [
            jnp.tile(eb, 8),
            jnp.tile(nb, 8),
            jnp.tile(cb, 4),
            jnp.tile(db, 4),
            jnp.tile(mb, 8),
            jnp.tile(ob, 8),
            jnp.zeros((256,), F32),
            jnp.zeros((256,), F32),
        ]
    )
    enter = jnp.tile(jnp.swapaxes(ew, 2, 3).reshape(18, 32), (1, 8))
    return (
        biases,
        enter,
        tap_tiles(nw, 8),
        tap_tiles(cw, 4),
        tap_tiles(dw, 4),
        tap_tiles(ow, 8),
        tap_tiles(fw, 128),
        jnp.tile(uw.T, (1, 8)),
        jnp.tile(sw.T, (1, 8)),
    )


def shards(
    sky_image,
    visibilities,
    grid_kernels,
    tile_counts,
    block_tiles,
    *parameters,
):
    slots = block_tiles.shape[2]
    live = jnp.arange(slots, dtype=jnp.int32) < jnp.sum(tile_counts[0, 0])
    owner = jnp.repeat(jnp.where(live, block_tiles[0, 0], -1), 64).reshape(1, slots * 64)
    vis = jnp.swapaxes(visibilities[0, 0], 0, 1).reshape(2, slots * 64)
    kernels = grid_kernels.reshape(slots * 64, 256)
    dirty, rows, cols = exchange(vis, owner, kernels, sky_image)
    return network(sky_image, dirty, rows, cols, network_weights(*parameters))


def solution(mesh):
    block = P("gx", "gy")
    return jax.shard_map(
        shards,
        mesh=mesh,
        in_specs=(
            block,
            P("gx", "gy", None, None, None),
            P("gx", "gy", None, None, None),
            P("gx", "gy", None),
            P("gx", "gy", None),
        )
        + (P(),) * 14,
        out_specs=(block, block),
        check_vma=False,
    )
```

```python
import functools
import math

import jax
import jax.numpy as jnp
import numpy as np
from jax import lax
from jax.experimental import pallas as pl
from jax.experimental.pallas import tpu as pltpu
from jax.sharding import PartitionSpec as P

MESH = pl.DeviceIdType.MESH
F32 = jnp.float32
BF16 = jnp.bfloat16

GE, GC, GM, GD, GO = 6, 6, 6, 6, 4
NX, NY = 32, 16
SLABS = 18
STRIPES = 16
PIX = SLABS * STRIPES
PIX2 = PIX // 2
GROUPS = 18


def dot(a, b):
    return jnp.dot(a, b, preferred_element_type=F32)


def dot_nt(a, b):
    return lax.dot_general(a, b, (((1,), (1,)), ((), ())), preferred_element_type=F32)


def complex_block(c, s):
    return np.stack([np.stack([c, -s]), np.stack([s, c])])


def transform_constants():
    turn = 2.0 * math.pi
    y0 = np.arange(128)
    cells = np.arange(256)
    ang = turn * (np.outer(y0, y0) % 128) / 128
    first = complex_block(np.cos(ang), np.sin(ang))
    first = first.reshape(2, 2, 128, 16, 8).transpose(0, 2, 3, 1, 4).reshape(256, 256)
    ang = turn * np.outer(y0, cells % 32) / 4096
    sign = np.where(y0 % 2 == 0, 1.0, -1.0)[:, None]
    twist1 = np.stack([np.cos(ang) * sign, np.sin(ang) * sign])
    short = np.arange(32)
    ang = turn * (np.outer(short, short) % 32) / 32
    c32, s32 = np.cos(ang), np.sin(ang)
    second = complex_block(c32, s32)
    second = np.einsum("abys,rt->yarbts", second, np.eye(8)).reshape(512, 512)
    third = complex_block(c32, s32)
    third = np.einsum("abxi,yz->ayxibz", third, np.eye(8)).reshape(512, 512)
    ang = turn * np.outer(y0, y0) / 4096
    twist2 = np.stack([np.cos(ang) * sign, np.sin(ang) * sign]) / 4096
    ang = turn * (np.outer(short, y0) % 32) / 32
    fourth = np.concatenate([np.cos(ang), -np.sin(ang)], axis=1)
    return (
        jnp.asarray(first, BF16),
        jnp.asarray(twist1, F32),
        jnp.asarray(second, BF16),
        jnp.asarray(third, BF16),
        jnp.asarray(twist2, F32),
        jnp.asarray(fourth, BF16),
        jnp.asarray(np.eye(128), BF16),
    )


def permutations():
    into = np.zeros((20, STRIPES, 384), np.float32)
    back = np.zeros((256, SLABS, STRIPES), np.float32)
    for w in range(-1, SLABS + 1):
        for s in range(STRIPES):
            col = SLABS * s + w - 8
            if 0 <= col < 264:
                into[w + 1, s, col] = 1
            elif -8 <= col < 0:
                into[w + 1, s, 384 + col] = 1
            if 0 <= col < 256 and 0 <= w < SLABS:
                back[col, w, s] = 1
    return jnp.asarray(into.reshape(320, 384), BF16), jnp.asarray(back.reshape(256, PIX), BF16)


def send_all(axis, count, me, source, landing, send_sem, recv_sem):
    def one(step, carry):
        other = lax.rem(me + step, count)
        pltpu.make_async_remote_copy(
            src_ref=source.at[other],
            dst_ref=landing.at[me],
            send_sem=send_sem,
            recv_sem=recv_sem,
            device_id={axis: other},
            device_id_type=MESH,
        ).start()
        return carry

    lax.fori_loop(1, count, one, 0)
    landing[me] = source[me]


def wait_bytes(ref, sem):
    pltpu.make_async_copy(ref, ref, sem).wait()


def grid_tiles(vis, counts, owner, kernels):
    wide = vis[...].astype(F32)
    parts = [jnp.concatenate([wide[:, k, :]] * 2, axis=1) for k in range(2)]
    slot = lax.broadcasted_iota(jnp.int32, (64, 128), 0)
    half = lax.broadcasted_iota(jnp.int32, (64, 128), 1) // 64
    contrib = None
    for piece in range(8):
        blocks = []
        for q in range(4 * piece, 4 * piece + 4):
            hit = slot == 2 * q + half
            block = [jnp.where(hit, part, 0.0).astype(BF16) for part in parts]
            blocks.append(jnp.concatenate(block, axis=0))
        term = dot(jnp.concatenate(blocks, axis=1), kernels[512 * piece : 512 * piece + 512, :])
        contrib = term if contrib is None else contrib + term
    live = jnp.sum(counts[...], axis=1, keepdims=True)
    both = jnp.concatenate([owner[...]] * 2, axis=1)
    lane = lax.broadcasted_iota(jnp.int32, (1, 128), 1) % 64
    both = jnp.where(lane < live, both, -1)
    chosen = jnp.where(lax.broadcasted_iota(jnp.int32, (128, 128), 0) == both, 1.0, 0.0)
    chosen = chosen.astype(BF16)
    sums = []
    for k in range(2):
        own = contrib[64 * k : 64 * k + 64]
        high = own.astype(BF16)
        low = (own - high.astype(F32)).astype(BF16)
        total = dot(chosen, jnp.concatenate([high, low], axis=0))
        sums.append(total.reshape(16, 8, 256))
    return jnp.concatenate(sums, axis=1).astype(BF16)


def column_transform(held, first, twist1, second):
    turned = dot(first[...], held)
    real, imag = turned[:128], turned[128:]
    c, s = twist1[0], twist1[1]
    both = jnp.concatenate([real * c - imag * s, real * s + imag * c], axis=1).astype(BF16)
    return dot_nt(second[...], both)


def columns_up(held, eye):
    wide = held.astype(F32).reshape(16, 4, 8, 128)
    halves = []
    for y1 in range(2):
        parts = []
        for part in range(2):
            piece = wide[:, 2 * y1 + part].reshape(128, 128).astype(BF16)
            parts.append(dot_nt(eye, piece).reshape(16, 8, 128))
        halves.append(jnp.concatenate(parts, axis=1))
    return jnp.concatenate(halves, axis=0).astype(BF16)


def row_transform(held, third, twist2, fourth, store):
    turned = dot(third[...], held)
    for y in range(8):
        real = turned[32 * y : 32 * y + 32]
        imag = turned[256 + 32 * y : 256 + 32 * y + 32]
        real = jnp.concatenate([real] * 4, axis=0)
        imag = jnp.concatenate([imag] * 4, axis=0)
        c, s = twist2[0], twist2[1]
        both = jnp.concatenate([real * c - imag * s, real * s + imag * c], axis=1).astype(BF16)
        store(y, dot_nt(fourth[...], both))


def repeat_matrix(rows):
    row = lax.broadcasted_iota(jnp.int32, (rows, 256), 0)
    lane = lax.broadcasted_iota(jnp.int32, (rows, 256), 1)
    return jnp.where(lane % rows == row, 1.0, 0.0).astype(BF16)


def dot_tn(a, b):
    return lax.dot_general(a, b, (((0,), (0,)), ((), ())), preferred_element_type=F32)


def band(dst, tile, high, rows, start, lane_id, count):
    for dc in range(3):
        taps = [tile(p, dc) for p in range(3)]
        for row in range(rows):
            block = None
            for p in range(3):
                out_row = row - start - p
                if 0 <= out_row < count:
                    term = jnp.where(lane_id == out_row, taps[p], 0.0)
                    block = term if block is None else block + term
            if block is None:
                block = jnp.zeros(lane_id.shape, F32)
            at = (dc * rows + row) * high
            dst[at : at + high, :] = block.astype(BF16)


def exchange_kernel(*refs):
    (
        first_h,
        twist1_h,
        second_h,
        third_h,
        twist2_h,
        fourth_h,
        eye_h,
        kernels_h,
        vis_h,
        counts_h,
        owner_h,
        sky_h,
    ) = refs[:12]
    weights_h = refs[12:26]
    dirty_out, rows_out, cols_out = refs[26:29]
    bands_out = refs[29:38]
    (
        first,
        twist1,
        second,
        third,
        twist2,
        fourth,
        eye,
        kernels,
        vis,
        counts,
        owner,
        sky,
    ) = refs[38:50]
    weights = refs[50:64]
    built = refs[64:73]
    w_enter, w_encode, w_coarse, w_deeper, w_decode, w_output, w_upward, w_skip, biases = built
    (
        tiles,
        landed1,
        bands,
        landed2,
        ups,
        landed3,
        image,
        downs,
        landed4,
        sides,
        sky_rows,
        sky_sides,
        sky_cols,
        sky_own,
        send_sem,
        recv_sem,
        load_sem,
        save_sem,
    ) = refs[73:]
    saves = [
        pltpu.make_async_copy(source, target, save_sem.at[k])
        for k, (source, target) in enumerate(zip(built, bands_out))
    ]
    save_rows = pltpu.make_async_copy(sky_rows, rows_out, save_sem.at[9])
    save_cols = pltpu.make_async_copy(sky_sides, cols_out, save_sem.at[10])
    save_main = pltpu.make_async_copy(landed4, dirty_out.at[pl.ds(0, 32)], save_sem.at[11])
    save_sides = pltpu.make_async_copy(sides, dirty_out.at[pl.ds(32, 2)], save_sem.at[12])
    gx, gy = lax.axis_index("gx"), lax.axis_index("gy")
    down_x, up_x = lax.rem(gx + 1, NX), lax.rem(gx + NX - 1, NX)
    right_y, left_y = lax.rem(gy + 1, NY), lax.rem(gy + NY - 1, NY)
    barrier = pltpu.get_barrier_semaphore()

    def greet(axis, count, me):
        def one(step, carry):
            pl.semaphore_signal(
                barrier, inc=1, device_id={axis: lax.rem(me + step, count)}, device_id_type=MESH
            )
            return carry

        lax.fori_loop(1, count, one, 0)

    greet("gy", NY, gy)
    greet("gx", NX, gx)
    for x, y in ((NX - 1, left_y), (0, right_y)):
        pl.semaphore_signal(barrier, inc=1, device_id={"gx": x, "gy": y}, device_id_type=MESH)

    sources = (kernels_h, vis_h, counts_h, owner_h, sky_h, first_h, twist1_h, second_h)
    sources += weights_h + (third_h, twist2_h, fourth_h, eye_h)
    targets = (kernels, vis, counts, owner, sky, first, twist1, second)
    targets += weights + (third, twist2, fourth, eye)
    loads = [
        pltpu.make_async_copy(source, target, load_sem.at[k])
        for k, (source, target) in enumerate(zip(sources, targets))
    ]
    for load in loads:
        load.start()

    for load in loads[:5]:
        load.wait()
    sky_own[...] = sky[...].astype(BF16)
    tiles[...] = grid_tiles(vis, counts, owner, kernels)
    edge = jnp.where((gx == 0) | (gx == NX - 1), NX, 0)
    pl.semaphore_wait(barrier, NX + NY - 2 + edge)

    send_all("gy", NY, gy, tiles, landed1, send_sem.at[0], recv_sem.at[0])

    def to_side(source, target, slot, axis, other):
        return pltpu.make_async_remote_copy(
            src_ref=source,
            dst_ref=target,
            send_sem=send_sem.at[slot],
            recv_sem=recv_sem.at[slot],
            device_id={axis: other},
            device_id_type=MESH,
        )

    row_copies = [
        to_side(sky_own.at[pl.ds(112, 16)], sky_rows.at[0], 4, "gx", down_x),
        to_side(sky_own.at[pl.ds(0, 16)], sky_rows.at[1], 5, "gx", up_x),
    ]
    for copy in row_copies:
        copy.start()

    for load in loads[5:]:
        load.wait()
    enter_w, encode_w, coarse_w, deeper_w, decode_w, output_w, upward_w, skip_w = weights[:8]
    rep32, rep64 = repeat_matrix(32), repeat_matrix(64)
    lane32 = lax.broadcasted_iota(jnp.int32, (32, 256), 1)
    lane64 = lax.broadcasted_iota(jnp.int32, (64, 256), 1)
    band(w_encode, lambda p, dc: dot_tn(encode_w[p, dc], rep32), 32, 16, 3, lane32 // 32, 8)
    saves[1].start()
    band(w_decode, lambda p, dc: dot_tn(decode_w[p, dc], rep32), 32, 16, 3, lane32 // 32, 8)
    saves[4].start()

    wait_bytes(landed1.at[pl.ds(0, 15)], recv_sem.at[0])
    turned = column_transform(landed1[...].reshape(256, 256), first, twist1, second)
    bands[...] = turned.astype(BF16).reshape(16, 32, 128)
    send_all("gy", NY, gy, bands, landed2, send_sem.at[1], recv_sem.at[1])

    for copy in row_copies:
        copy.wait()
    for half in range(2):
        lanes = slice(128 * half, 128 * half + 128)
        sky_cols[half, 0:16] = sky_rows[0, :, lanes]
        sky_cols[half, 16:144] = sky_own[:, lanes]
        sky_cols[half, 144:160] = sky_rows[1, :, lanes]
    col_copies = [
        to_side(sky_cols.at[1], sky_sides.at[0], 6, "gy", right_y),
        to_side(sky_cols.at[0], sky_sides.at[1], 7, "gy", left_y),
    ]
    for copy in col_copies:
        copy.start()

    band(w_coarse, lambda p, dc: dot(coarse_w[p, dc], rep64), 32, 12, 3, lane32 // 64, 4)
    saves[2].start()
    band(w_deeper, lambda p, dc: dot_tn(deeper_w[p, dc], rep64), 64, 8, 1, lane64 // 64, 4)
    saves[3].start()
    lane_out = lax.broadcasted_iota(jnp.int32, (32, 128), 1)
    tap_row = lax.broadcasted_iota(jnp.int32, (3, 128), 0)

    def output_tile(p, dc):
        return dot_tn(output_w[p], jnp.where(tap_row == dc, 1.0, 0.0).astype(BF16))

    band(w_output, output_tile, 32, 16, 3, lane_out % 8, 8)
    saves[5].start()

    wait_bytes(landed2.at[pl.ds(0, 15)], recv_sem.at[1])
    ups[...] = columns_up(landed2[...], eye[...])
    send_all("gx", NX, gx, ups, landed3, send_sem.at[2], recv_sem.at[2])

    lifted = dot_tn(upward_w[...], rep32)
    for row in range(4):
        block = jnp.where(lane64 // 64 == row, lifted, 0.0)
        w_upward[64 * row : 64 * row + 64, :] = block.astype(BF16)
    skipped = dot_tn(skip_w[...], rep32)
    for row in range(8):
        block = jnp.where(lane32 // 32 == row, skipped, 0.0)
        w_skip[32 * row : 32 * row + 32, :] = block.astype(BF16)
    row_id = lax.broadcasted_iota(jnp.int32, (64, 256), 0)
    for dc in range(3):
        taps = [dot(enter_w[p, dc], rep32) for p in range(3)]
        for variant in range(4):
            for channel in range(2):
                block = jnp.zeros((64, 256), F32)
                for p in range(3):
                    hit = row_id - 15 - 8 * variant - p == lane64 // 32
                    block = block + jnp.where(hit, taps[p][channel : channel + 1, :], 0.0)
                at = dc * 128 + channel * 64
                w_enter[variant, at : at + 64, :] = block.astype(BF16)
    for row, ref in enumerate(weights[8:]):
        biases[row : row + 1, :] = jnp.concatenate([ref[...]] * (256 // ref.shape[1]), axis=1)
    biases[6:8, :] = jnp.zeros((2, 256), F32)
    for k in (0, 6, 7, 8):
        saves[k].start()

    def store(y, value):
        image[pl.ds(8 + y, 32, stride=8), :] = value

    image[0:8] = jnp.zeros((8, 128), F32)
    image[264:272] = jnp.zeros((8, 128), F32)

    wait_bytes(landed3.at[pl.ds(0, 31)], recv_sem.at[2])
    row_transform(landed3[...].reshape(512, 128), third, twist2, fourth, store)
    whole = image[...].reshape(34, 8, 128)
    lane = lax.broadcasted_iota(jnp.int32, (32, 8, 128), 2)
    outer = jnp.where(lane < 64, whole[2:34], whole[0:32])
    downs[...] = jnp.concatenate([whole[1:33], outer], axis=1).astype(BF16)
    send_all("gx", NX, gx, downs, landed4, send_sem.at[3], recv_sem.at[3])

    def beside(other_y, slot):
        def one(x, carry):
            pltpu.make_async_remote_copy(
                src_ref=downs.at[x],
                dst_ref=sides.at[slot],
                send_sem=send_sem.at[8 + slot],
                recv_sem=recv_sem.at[8 + slot],
                device_id={"gx": x, "gy": other_y},
                device_id_type=MESH,
            ).start()
            return carry

        lax.fori_loop(0, NX, one, 0)

    @pl.when(gx == NX - 1)
    def _():
        beside(right_y, 0)

    @pl.when(gx == 0)
    def _():
        beside(left_y, 1)

    for copy in col_copies:
        copy.wait()
    save_rows.start()
    save_cols.start()

    wait_bytes(landed4.at[pl.ds(0, 31)], recv_sem.at[3])
    save_main.start()
    wait_bytes(sides.at[0], recv_sem.at[8])
    wait_bytes(sides.at[1], recv_sem.at[9])
    save_sides.start()
    for save in saves + [save_rows, save_cols]:
        save.wait()
    save_main.wait()
    save_sides.wait()
    wait_bytes(tiles.at[pl.ds(0, 15)], send_sem.at[0])
    wait_bytes(bands.at[pl.ds(0, 15)], send_sem.at[1])
    wait_bytes(ups.at[pl.ds(0, 31)], send_sem.at[2])
    wait_bytes(downs.at[pl.ds(0, 31)], send_sem.at[3])

    @pl.when(gx == NX - 1)
    def _():
        wait_bytes(downs, send_sem.at[8])

    @pl.when(gx == 0)
    def _():
        wait_bytes(downs, send_sem.at[9])


def exchange(vis, counts, owner, kernels, sky, weights):
    hbm = pl.BlockSpec(memory_space=pltpu.HBM)
    operands = transform_constants() + (kernels, vis, counts, owner, sky) + weights
    shapes = [
        (34, 16, 128),
        (2, 16, 256),
        (2, 160, 128),
        (4, 384, 256),
        (1536, 256),
        (1152, 256),
        (1536, 256),
        (1536, 256),
        (1536, 128),
        (256, 256),
        (256, 256),
    ]
    outs = [jax.ShapeDtypeStruct(shape, BF16) for shape in shapes]
    outs.append(jax.ShapeDtypeStruct((8, 256), F32))
    return pl.pallas_call(
        exchange_kernel,
        out_shape=tuple(outs),
        in_specs=[hbm] * len(operands),
        out_specs=(hbm,) * len(outs),
        scratch_shapes=[pltpu.VMEM(x.shape, x.dtype) for x in list(operands) + outs[3:]]
        + [
            pltpu.VMEM((16, 16, 256), BF16),
            pltpu.VMEM((16, 16, 256), BF16),
            pltpu.VMEM((16, 32, 128), BF16),
            pltpu.VMEM((16, 32, 128), BF16),
            pltpu.VMEM((32, 16, 128), BF16),
            pltpu.VMEM((32, 16, 128), BF16),
            pltpu.VMEM((272, 128), F32),
            pltpu.VMEM((32, 16, 128), BF16),
            pltpu.VMEM((32, 16, 128), BF16),
            pltpu.VMEM((2, 16, 128), BF16),
            pltpu.VMEM((2, 16, 256), BF16),
            pltpu.VMEM((2, 160, 128), BF16),
            pltpu.VMEM((2, 160, 128), BF16),
            pltpu.VMEM((128, 256), BF16),
            pltpu.SemaphoreType.DMA((10,)),
            pltpu.SemaphoreType.DMA((10,)),
            pltpu.SemaphoreType.DMA((len(operands),)),
            pltpu.SemaphoreType.DMA((13,)),
        ],
        compiler_params=pltpu.CompilerParams(
            collective_id=0, has_side_effects=True, vmem_limit_bytes=64 << 20
        ),
        name="exchange",
    )(*operands)


def network_kernel(*refs):
    sources, (dirty_out, estimate_out), targets = refs[:16], refs[16:18], refs[18:34]
    window, entry, fine_a, fine_b, fine_c, pooled, coarse, mask, w_pool, drawn, load_sem = refs[34:]
    loads = [
        pltpu.make_async_copy(source, target, load_sem.at[k])
        for k, (source, target) in enumerate(zip(sources, targets))
    ]
    for load in loads:
        load.start()
    sky, dirty_in, rows_in, cols_in, eye, into, w_enter, biases = targets[:8]
    w_encode, w_coarse, w_deeper, w_upward, w_skip, w_decode, w_output, back = targets[8:]

    def arrived(first, last):
        for load in loads[first:last]:
            load.wait()

    gx, gy = lax.axis_index("gx"), lax.axis_index("gy")
    last_x, last_y = lax.axis_size("gx") - 1, lax.axis_size("gy") - 1
    keep_top = jnp.where(gx == 0, 0.0, 1.0).astype(F32)
    keep_bottom = jnp.where(gx == last_x, 0.0, 1.0).astype(F32)

    rows512 = lax.broadcasted_iota(jnp.int32, (512, 128), 0)
    lanes512 = lax.broadcasted_iota(jnp.int32, (512, 128), 1)
    pairs = ((rows512 % 256) // 64 == lanes512 // 32) & (rows512 % 32 == lanes512 % 32)
    w_pool[...] = jnp.where(pairs, 0.25, 0.0).astype(BF16)
    slab = lax.broadcasted_iota(jnp.int32, (20, 16, 128), 0)
    stripe = lax.broadcasted_iota(jnp.int32, (20, 16, 128), 1)
    col = SLABS * stripe + slab - 9 + 256 * gy
    mask[...] = jnp.where((col >= 0) & (col < 256 * (last_y + 1)), 1.0, 0.0).astype(F32)

    arrived(0, 6)
    lane = lax.broadcasted_iota(jnp.int32, (160, 128), 1)
    beside = jnp.where(lane < 64, cols_in[1].astype(F32), cols_in[0].astype(F32))
    above = rows_in[0].astype(F32)[8:16] * keep_top
    below = rows_in[1].astype(F32)[0:8] * keep_bottom
    zeros = jnp.zeros((32, 256), F32)
    window[0, :, 0:256] = jnp.concatenate(
        [zeros[:16], above, sky[...], below, zeros], axis=0
    ).astype(BF16)
    beside = jnp.concatenate(
        [
            zeros[:16, :128],
            beside[8:16] * keep_top,
            beside[16:144],
            beside[144:152] * keep_bottom,
            zeros[:, :128],
        ],
        axis=0,
    )
    window[0, :, 256:384] = beside.astype(BF16)
    wide = dirty_in[...].astype(F32)
    gap = jnp.zeros((112, 128), F32)
    parts = []
    for half in range(2):
        rows8 = slice(8 * half, 8 * half + 8)
        stacked = jnp.concatenate(
            [wide[0:32, rows8].reshape(256, 128), wide[33, rows8], gap, wide[32, rows8]], axis=0
        )
        parts.append(dot_nt(eye[...], stacked.astype(BF16)))
    dirty_out[...] = parts[0][:, 0:256]
    zeros = jnp.zeros((32, 384), F32)
    window[1] = jnp.concatenate(
        [zeros[:16], parts[1][120:128] * keep_top, parts[0], parts[1][0:8] * keep_bottom, zeros],
        axis=0,
    ).astype(BF16)
    for q in range(5):
        rows64 = slice(32 * q, 32 * q + 64)
        both = jnp.concatenate([window[0, rows64], window[1, rows64]], axis=0)
        placed = dot_nt(into[...], both).reshape(20, 16, 128) * mask[...]
        entry[q] = placed.astype(BF16)

    blank = jnp.zeros((20, 16, 128), BF16)
    for ref, top in ((fine_a, 37), (fine_b, 37), (fine_c, 37), (pooled, 19), (coarse, 37)):
        ref[0] = blank[: ref.shape[1]]
        ref[top] = blank[: ref.shape[1]]

    def row_keep(group):
        top = jnp.where(group == 0, keep_top, 1.0)
        bottom = jnp.where(group == GROUPS - 1, keep_bottom, 1.0)
        return top * bottom

    def put(ref, at, value, slabs):
        ref[at, 1 : slabs + 1] = value.astype(BF16)
        ref[at, 0] = pltpu.roll(value[slabs - 1], 1, 0).astype(BF16)
        ref[at, slabs + 1] = pltpu.roll(value[0], STRIPES - 1, 0).astype(BF16)

    def finish(total, bias_row, keep):
        value = jnp.maximum(total + biases[bias_row : bias_row + 1, :], 0.0)
        scaled = mask[1:19] * keep
        return [
            value[:, 128 * h : 128 * h + 128].reshape(SLABS, 16, 128) * scaled for h in range(2)
        ]

    def gathered(ref, at, high, slabs, stride, count):
        pieces = []
        for dc in range(3):
            for h in range(high):
                rows = [
                    ref[at + stride * g + h, dc : dc + slabs].reshape(slabs * 16, 128)
                    for g in range(count)
                ]
                pieces.append(jnp.concatenate(rows, axis=0))
        return jnp.concatenate(pieces, axis=1)

    arrived(6, 8)
    for variant in range(4):
        members = list(range(variant, GROUPS, 4))
        pieces = []
        for dc in range(3):
            rows = [entry[group // 4, dc : dc + SLABS].reshape(PIX, 128) for group in members]
            pieces.append(jnp.concatenate(rows, axis=0))
        total = dot(jnp.concatenate(pieces, axis=1), w_enter[variant])
        for g, group in enumerate(members):
            for h, value in enumerate(finish(total[PIX * g : PIX * g + PIX], 0, row_keep(group))):
                put(fine_a, 2 * group + 1 + h, value, SLABS)

    def encode_step(step, carry):
        total = dot(gathered(fine_a, 2 * GE * step, 4, SLABS, 2, GE), w_encode[...])
        columns = [[], [], [], []]
        for g in range(GE):
            group = GE * step + g
            for h, value in enumerate(finish(total[PIX * g : PIX * g + PIX], 1, row_keep(group))):
                put(fine_b, 2 * group + 1 + h, value, SLABS)
                split = value.reshape(SLABS // 2, 2, 16, 128)
                columns[h].append(split[:, 0].reshape(PIX2, 128).astype(BF16))
                columns[2 + h].append(split[:, 1].reshape(PIX2, 128).astype(BF16))
        both = jnp.concatenate([jnp.concatenate(c, axis=0) for c in columns], axis=1)
        small = dot(both, w_pool[...])
        for g in range(GE):
            value = small[PIX2 * g : PIX2 * g + PIX2].reshape(SLABS // 2, 16, 128)
            put(pooled, GE * step + g + 1, value, SLABS // 2)
        return carry

    arrived(8, 9)
    lax.fori_loop(0, GROUPS // GE, encode_step, 0)

    even_mask = mask[1:19].reshape(SLABS // 2, 2, 16, 128)[:, 0]

    def coarse_step(step, carry):
        total = dot(gathered(pooled, GC * step, 3, SLABS // 2, 1, GC), w_coarse[...])
        for g in range(GC):
            group = GC * step + g
            value = jnp.maximum(total[PIX2 * g : PIX2 * g + PIX2] + biases[2:3, :], 0.0)
            scaled = even_mask * row_keep(group)
            for h in range(2):
                half = value[:, 128 * h : 128 * h + 128].reshape(SLABS // 2, 16, 128) * scaled
                put(coarse, 2 * group + 1 + h, half, SLABS // 2)
        return carry

    arrived(9, 10)
    lax.fori_loop(0, GROUPS // GC, coarse_step, 0)

    def merge_step(step, carry):
        total = dot(gathered(coarse, 2 * GM * step, 4, SLABS // 2, 2, GM), w_deeper[...])
        value = jnp.maximum(total + biases[3:4, :], 0.0).astype(BF16)
        lifted = dot(value, w_upward[...]).reshape(GM, SLABS // 2, 1, 16, 256)
        halves = []
        for h in range(2):
            rows = [
                fine_b[2 * (GM * step + g) + 1 + h, 1:19].reshape(PIX, 128) for g in range(GM)
            ]
            halves.append(jnp.concatenate(rows, axis=0))
        skipped = dot(jnp.concatenate(halves, axis=1), w_skip[...])
        total = skipped.reshape(GM, SLABS // 2, 2, 16, 256) + lifted
        total = total.reshape(GM * PIX, 256)
        for g in range(GM):
            group = GM * step + g
            for h, half in enumerate(finish(total[PIX * g : PIX * g + PIX], 4, row_keep(group))):
                put(fine_a, 2 * group + 1 + h, half, SLABS)
        return carry

    arrived(10, 13)
    lax.fori_loop(0, GROUPS // GM, merge_step, 0)

    def decode_step(step, carry):
        total = dot(gathered(fine_a, 2 * GD * step, 4, SLABS, 2, GD), w_decode[...])
        for g in range(GD):
            group = GD * step + g
            for h, half in enumerate(finish(total[PIX * g : PIX * g + PIX], 5, row_keep(group))):
                put(fine_c, 2 * group + 1 + h, half, SLABS)
        return carry

    arrived(13, 14)
    lax.fori_loop(0, GROUPS // GD, decode_step, 0)

    lane_row = lax.broadcasted_iota(jnp.int32, (PIX, 128), 1) // 8

    def output_step(step, carry):
        total = dot(gathered(fine_c, 2 + 2 * GO * step, 4, SLABS, 2, GO), w_output[...])
        kept = drawn[...]
        for g in range(GO):
            kept = jnp.where(lane_row == GO * step + g, total[PIX * g : PIX * g + PIX], kept)
        drawn[...] = kept
        return carry

    drawn[...] = jnp.zeros((PIX, 128), F32)
    arrived(14, 16)
    lax.fori_loop(0, 16 // GO, output_step, 0)

    update = drawn[...]
    high = update.astype(BF16)
    low = (update - high.astype(F32)).astype(BF16)
    ordered = dot(back[...], high) + dot(back[...], low)
    estimate_out[...] = sky[...] + ordered.T


def network(sky, dirty_in, rows_in, cols_in, bands):
    vmem, hbm = pl.BlockSpec(memory_space=pltpu.VMEM), pl.BlockSpec(memory_space=pltpu.HBM)
    into, back = permutations()
    eye = jnp.asarray(np.eye(128), BF16)
    enter, encode, coarse, deeper, decode, output, upward, skip, biases = bands
    operands = (sky, dirty_in, rows_in, cols_in, eye, into, enter, biases)
    operands += (encode, coarse, deeper, upward, skip, decode, output, back)
    return pl.pallas_call(
        network_kernel,
        out_shape=(
            jax.ShapeDtypeStruct((128, 256), F32),
            jax.ShapeDtypeStruct((128, 256), F32),
        ),
        in_specs=[hbm] * len(operands),
        out_specs=(vmem, vmem),
        scratch_shapes=[pltpu.VMEM(x.shape, x.dtype) for x in operands]
        + [
            pltpu.VMEM((2, 192, 384), BF16),
            pltpu.VMEM((5, 20, 16, 128), BF16),
            pltpu.VMEM((38, 20, 16, 128), BF16),
            pltpu.VMEM((38, 20, 16, 128), BF16),
            pltpu.VMEM((38, 20, 16, 128), BF16),
            pltpu.VMEM((20, 11, 16, 128), BF16),
            pltpu.VMEM((38, 11, 16, 128), BF16),
            pltpu.VMEM((20, 16, 128), F32),
            pltpu.VMEM((512, 128), BF16),
            pltpu.VMEM((PIX, 128), F32),
            pltpu.SemaphoreType.DMA((len(operands),)),
        ],
        compiler_params=pltpu.CompilerParams(vmem_limit_bytes=64 << 20),
        name="network",
    )(*operands)


def raw_weights(ew, eb, nw, nb, cw, cb, dw, db, uw, sw, mb, ow, ob, fw):
    biases = tuple(b.reshape(1, -1) for b in (eb, nb, cb, db, mb, ob))
    return (
        jnp.swapaxes(ew, 2, 3),
        nw,
        jnp.swapaxes(cw, 2, 3),
        dw,
        ow,
        fw[:, :, 0, :],
        uw,
        sw,
    ) + biases


def shards(
    sky_image,
    visibilities,
    grid_kernels,
    tile_counts,
    block_tiles,
    *parameters,
):
    slots = block_tiles.shape[2]
    dirty, rows, cols, *bands = exchange(
        visibilities[0, 0],
        tile_counts.reshape(1, -1),
        block_tiles.reshape(1, -1),
        grid_kernels.reshape(slots * 64, 256),
        sky_image,
        raw_weights(*parameters),
    )
    return network(sky_image, dirty, rows, cols, tuple(bands))


def solution(mesh):
    block = P("gx", "gy")
    return jax.shard_map(
        shards,
        mesh=mesh,
        in_specs=(
            block,
            P("gx", "gy", None, None, None),
            P("gx", "gy", None, None, None),
            P("gx", "gy", None),
            P("gx", "gy", None),
        )
        + (P(),) * 14,
        out_specs=(block, block),
        check_vma=False,
    )
```

```python
import functools
import math

import jax
import jax.numpy as jnp
import numpy as np
from jax import lax
from jax.experimental import pallas as pl
from jax.experimental.pallas import tpu as pltpu
from jax.sharding import PartitionSpec as P

MESH = pl.DeviceIdType.MESH
F32 = jnp.float32
BF16 = jnp.bfloat16

GE, GC, GM, GD = 9, 9, 9, 9
NX, NY = 32, 16
SLABS = 18
STRIPES = 16
PIX = SLABS * STRIPES
PIX2 = PIX // 2
GROUPS = 18


def dot(a, b):
    return jnp.dot(a, b, preferred_element_type=F32)


def dot_nt(a, b):
    return lax.dot_general(a, b, (((1,), (1,)), ((), ())), preferred_element_type=F32)


def complex_block(c, s):
    return np.stack([np.stack([c, -s]), np.stack([s, c])])


def transform_constants():
    turn = 2.0 * math.pi
    y0 = np.arange(128)
    cells = np.arange(256)
    ang = turn * (np.outer(y0, y0) % 128) / 128
    first = complex_block(np.cos(ang), np.sin(ang))
    first = first.reshape(2, 2, 128, 16, 8).transpose(0, 2, 3, 1, 4).reshape(256, 256)
    ang = turn * np.outer(y0, cells % 32) / 4096
    sign = np.where(y0 % 2 == 0, 1.0, -1.0)[:, None]
    twist1 = np.stack([np.cos(ang) * sign, np.sin(ang) * sign])
    short = np.arange(32)
    ang = turn * (np.outer(short, short) % 32) / 32
    c32, s32 = np.cos(ang), np.sin(ang)
    second = complex_block(c32, s32)
    second = np.einsum("abys,rt->yarbts", second, np.eye(8)).reshape(512, 512)
    third = complex_block(c32, s32)
    third = np.einsum("abxi,yz->ayxibz", third, np.eye(8)).reshape(512, 512)
    ang = turn * np.outer(y0, y0) / 4096
    twist2 = np.stack([np.cos(ang) * sign, np.sin(ang) * sign]) / 4096
    ang = turn * (np.outer(short, y0) % 32) / 32
    fourth = np.concatenate([np.cos(ang), -np.sin(ang)], axis=1)
    return (
        jnp.asarray(first, BF16),
        jnp.asarray(twist1, F32),
        jnp.asarray(second, BF16),
        jnp.asarray(third, BF16),
        jnp.asarray(twist2, F32),
        jnp.asarray(fourth, BF16),
        jnp.asarray(np.eye(128), BF16),
    )


def permutations():
    into = np.zeros((20, STRIPES, 384), np.float32)
    back = np.zeros((256, SLABS, STRIPES), np.float32)
    for w in range(-1, SLABS + 1):
        for s in range(STRIPES):
            col = SLABS * s + w - 8
            if 0 <= col < 264:
                into[w + 1, s, col] = 1
            elif -8 <= col < 0:
                into[w + 1, s, 384 + col] = 1
            if 0 <= col < 256 and 0 <= w < SLABS:
                back[col, w, s] = 1
    return jnp.asarray(into.reshape(320, 384), BF16), jnp.asarray(back.reshape(256, PIX), BF16)


def send_all(axis, count, me, source, landing, send_sem, recv_sem):
    def one(step, carry):
        away = (step + 1) // 2
        shift = count // 2 + jnp.where(step % 2 == 1, away, -away)
        other = lax.rem(me + shift, count)
        pltpu.make_async_remote_copy(
            src_ref=source.at[other],
            dst_ref=landing.at[me],
            send_sem=send_sem,
            recv_sem=recv_sem,
            device_id={axis: other},
            device_id_type=MESH,
        ).start()
        return carry

    lax.fori_loop(0, count - 1, one, 0)
    landing[me] = source[me]


def wait_bytes(ref, sem):
    pltpu.make_async_copy(ref, ref, sem).wait()


def grid_tiles(vis, counts, owner, kernels):
    wide = vis[...].astype(F32)
    parts = [jnp.concatenate([wide[:, k, :]] * 2, axis=1) for k in range(2)]
    slot = lax.broadcasted_iota(jnp.int32, (64, 128), 0)
    half = lax.broadcasted_iota(jnp.int32, (64, 128), 1) // 64
    contrib = None
    for piece in range(8):
        blocks = []
        for q in range(4 * piece, 4 * piece + 4):
            hit = slot == 2 * q + half
            block = [jnp.where(hit, part, 0.0).astype(BF16) for part in parts]
            blocks.append(jnp.concatenate(block, axis=0))
        term = dot(jnp.concatenate(blocks, axis=1), kernels[512 * piece : 512 * piece + 512, :])
        contrib = term if contrib is None else contrib + term
    live = jnp.sum(counts[...], axis=1, keepdims=True)
    both = jnp.concatenate([owner[...]] * 2, axis=1)
    lane = lax.broadcasted_iota(jnp.int32, (1, 128), 1) % 64
    both = jnp.where(lane < live, both, -1)
    chosen = jnp.where(lax.broadcasted_iota(jnp.int32, (128, 128), 0) == both, 1.0, 0.0)
    chosen = chosen.astype(BF16)
    sums = []
    for k in range(2):
        own = contrib[64 * k : 64 * k + 64]
        high = own.astype(BF16)
        low = (own - high.astype(F32)).astype(BF16)
        total = dot(chosen, jnp.concatenate([high, low], axis=0))
        sums.append(total.reshape(16, 8, 256))
    return jnp.concatenate(sums, axis=1).astype(BF16)


def column_transform(held, first, twist1, second):
    turned = dot(first[...], held)
    real, imag = turned[:128], turned[128:]
    c, s = twist1[0], twist1[1]
    both = jnp.concatenate([real * c - imag * s, real * s + imag * c], axis=1).astype(BF16)
    return dot_nt(second[...], both)


def columns_up(held, eye):
    wide = held.astype(F32).reshape(16, 4, 8, 128)
    halves = []
    for y1 in range(2):
        parts = []
        for part in range(2):
            piece = wide[:, 2 * y1 + part].reshape(128, 128).astype(BF16)
            parts.append(dot_nt(eye, piece).reshape(16, 8, 128))
        halves.append(jnp.concatenate(parts, axis=1))
    return jnp.concatenate(halves, axis=0).astype(BF16)


def row_transform(held, third, twist2, fourth, store):
    turned = dot(third[...], held)
    for y in range(8):
        real = turned[32 * y : 32 * y + 32]
        imag = turned[256 + 32 * y : 256 + 32 * y + 32]
        real = jnp.concatenate([real] * 4, axis=0)
        imag = jnp.concatenate([imag] * 4, axis=0)
        c, s = twist2[0], twist2[1]
        both = jnp.concatenate([real * c - imag * s, real * s + imag * c], axis=1).astype(BF16)
        store(y, dot_nt(fourth[...], both))


def repeat_matrix(rows):
    row = lax.broadcasted_iota(jnp.int32, (rows, 256), 0)
    lane = lax.broadcasted_iota(jnp.int32, (rows, 256), 1)
    return jnp.where(lane % rows == row, 1.0, 0.0).astype(BF16)


def dot_tn(a, b):
    return lax.dot_general(a, b, (((0,), (0,)), ((), ())), preferred_element_type=F32)


def band(dst, tile, high, rows, out_row, place, lane_id, count):
    for dc in range(3):
        taps = [tile(p, dc) for p in range(3)]
        for row in rows:
            block = jnp.zeros(lane_id.shape, F32)
            for p in range(3):
                if 0 <= out_row(row, p) < count:
                    block = block + jnp.where(lane_id == out_row(row, p), taps[p], 0.0)
            at = place(dc, row)
            dst[at : at + high, :] = block.astype(BF16)


def place_fine(dc, row):
    if row == 3:
        return (800, 864, 992)[dc]
    if row == 12:
        return (832, 768, 896)[dc]
    return 256 * dc + 32 * (row - 4)


def place_coarse(dc, row):
    if row < 4:
        return 768 + 128 * dc + 64 + 32 * (row - 2)
    if row > 11:
        return 768 + 128 * dc + 32 * (row - 12)
    return 256 * dc + 32 * (row - 4)


def place_deeper(dc, row):
    if row == 1:
        return 768 + 128 * dc + 64
    if row == 6:
        return 768 + 128 * dc
    return 256 * dc + 64 * (row - 2)


def exchange_kernel(*refs):
    (
        first_h,
        twist1_h,
        second_h,
        third_h,
        twist2_h,
        fourth_h,
        eye_h,
        kernels_h,
        vis_h,
        counts_h,
        owner_h,
        sky_h,
    ) = refs[:12]
    weights_h = refs[12:26]
    dirty_out, rows_out, cols_out = refs[26:29]
    bands_out = refs[29:38]
    (
        first,
        twist1,
        second,
        third,
        twist2,
        fourth,
        eye,
        kernels,
        vis,
        counts,
        owner,
        sky,
    ) = refs[38:50]
    weights = refs[50:64]
    built = refs[64:73]
    w_enter, w_encode, w_coarse, w_deeper, w_decode, w_output, w_upward, w_skip, biases = built
    (
        tiles,
        landed1,
        bands,
        landed2,
        ups,
        landed3,
        image,
        downs,
        landed4,
        sides,
        sky_rows,
        sky_sides,
        sky_cols,
        sky_own,
        send_sem,
        recv_sem,
        load_sem,
        save_sem,
    ) = refs[73:]
    saves = [
        pltpu.make_async_copy(source, target, save_sem.at[k])
        for k, (source, target) in enumerate(zip(built, bands_out))
    ]
    save_rows = pltpu.make_async_copy(sky_rows, rows_out, save_sem.at[9])
    save_cols = pltpu.make_async_copy(sky_sides, cols_out, save_sem.at[10])
    save_main = pltpu.make_async_copy(landed4, dirty_out.at[pl.ds(0, 32)], save_sem.at[11])
    save_sides = pltpu.make_async_copy(sides, dirty_out.at[pl.ds(32, 2)], save_sem.at[12])
    gx, gy = lax.axis_index("gx"), lax.axis_index("gy")
    down_x, up_x = lax.rem(gx + 1, NX), lax.rem(gx + NX - 1, NX)
    right_y, left_y = lax.rem(gy + 1, NY), lax.rem(gy + NY - 1, NY)
    barrier = pltpu.get_barrier_semaphore()

    def greet(axis, count, me):
        def one(step, carry):
            pl.semaphore_signal(
                barrier, inc=1, device_id={axis: lax.rem(me + step, count)}, device_id_type=MESH
            )
            return carry

        lax.fori_loop(1, count, one, 0)

    greet("gy", NY, gy)
    greet("gx", NX, gx)
    for x, y in ((NX - 1, left_y), (0, right_y)):
        pl.semaphore_signal(barrier, inc=1, device_id={"gx": x, "gy": y}, device_id_type=MESH)

    sources = (kernels_h, vis_h, counts_h, owner_h, sky_h, first_h, twist1_h, second_h)
    sources += weights_h + (third_h, twist2_h, fourth_h, eye_h)
    targets = (kernels, vis, counts, owner, sky, first, twist1, second)
    targets += weights + (third, twist2, fourth, eye)
    loads = [
        pltpu.make_async_copy(source, target, load_sem.at[k])
        for k, (source, target) in enumerate(zip(sources, targets))
    ]
    for load in loads:
        load.start()

    for load in loads[:5]:
        load.wait()
    sky_own[...] = sky[...].astype(BF16)
    tiles[...] = grid_tiles(vis, counts, owner, kernels)
    edge = jnp.where((gx == 0) | (gx == NX - 1), NX, 0)
    pl.semaphore_wait(barrier, NX + NY - 2 + edge)

    send_all("gy", NY, gy, tiles, landed1, send_sem.at[0], recv_sem.at[0])

    def to_side(source, target, slot, axis, other):
        return pltpu.make_async_remote_copy(
            src_ref=source,
            dst_ref=target,
            send_sem=send_sem.at[slot],
            recv_sem=recv_sem.at[slot],
            device_id={axis: other},
            device_id_type=MESH,
        )

    row_copies = [
        to_side(sky_own.at[pl.ds(112, 16)], sky_rows.at[0], 4, "gx", down_x),
        to_side(sky_own.at[pl.ds(0, 16)], sky_rows.at[1], 5, "gx", up_x),
    ]
    for copy in row_copies:
        copy.start()

    for load in loads[5:]:
        load.wait()
    enter_w, encode_w, coarse_w, deeper_w, decode_w, output_w, upward_w, skip_w = weights[:8]
    rep32, rep64 = repeat_matrix(32), repeat_matrix(64)
    lane32 = lax.broadcasted_iota(jnp.int32, (32, 256), 1)
    lane64 = lax.broadcasted_iota(jnp.int32, (64, 256), 1)
    rows = range(3, 13)

    def fine_row(row, p):
        return row - 3 - p

    for dst, raw, save in ((w_encode, encode_w, saves[1]), (w_decode, decode_w, saves[4])):
        dst[928:992, :] = jnp.zeros((64, 256), BF16)

        def tile(p, dc, raw=raw):
            return dot_tn(raw[p, dc], rep32)

        band(dst, tile, 32, rows, fine_row, place_fine, lane32 // 32, 8)
        save.start()

    wait_bytes(landed1.at[pl.ds(0, 15)], recv_sem.at[0])
    turned = column_transform(landed1[...].reshape(256, 256), first, twist1, second)
    bands[...] = turned.astype(BF16).reshape(16, 32, 128)
    send_all("gy", NY, gy, bands, landed2, send_sem.at[1], recv_sem.at[1])

    for copy in row_copies:
        copy.wait()
    for half in range(2):
        lanes = slice(128 * half, 128 * half + 128)
        sky_cols[half, 0:16] = sky_rows[0, :, lanes]
        sky_cols[half, 16:144] = sky_own[:, lanes]
        sky_cols[half, 144:160] = sky_rows[1, :, lanes]
    col_copies = [
        to_side(sky_cols.at[1], sky_sides.at[0], 6, "gy", right_y),
        to_side(sky_cols.at[0], sky_sides.at[1], 7, "gy", left_y),
    ]
    for copy in col_copies:
        copy.start()

    def coarse_tile(p, dc):
        return dot(coarse_w[p, dc], rep64)

    def coarse_row(row, p):
        return row // 2 - 1 - p

    band(w_coarse, coarse_tile, 32, range(2, 14), coarse_row, place_coarse, lane32 // 64, 4)
    saves[2].start()

    def deeper_tile(p, dc):
        return dot_tn(deeper_w[p, dc], rep64)

    def deeper_row(row, p):
        return row - 1 - p

    band(w_deeper, deeper_tile, 64, range(1, 7), deeper_row, place_deeper, lane64 // 64, 4)
    saves[3].start()
    tap_row = lax.broadcasted_iota(jnp.int32, (3, 256), 0)
    tap_lane = lax.broadcasted_iota(jnp.int32, (3, 256), 1) // 64
    own = jnp.where(tap_row == tap_lane, 1.0, 0.0).astype(BF16)
    taps = [dot_tn(output_w[p], own) for p in range(3)]
    for row in range(16):
        block = jnp.zeros((32, 256), F32)
        for p in range(3):
            if 0 <= row - 3 - p < 8:
                block = block + jnp.where(lane32 % 8 == row - 3 - p, taps[p], 0.0)
        w_output[32 * row : 32 * row + 32, :] = block.astype(BF16)
    saves[5].start()

    wait_bytes(landed2.at[pl.ds(0, 15)], recv_sem.at[1])
    ups[...] = columns_up(landed2[...], eye[...])
    send_all("gx", NX, gx, ups, landed3, send_sem.at[2], recv_sem.at[2])

    lifted = dot_tn(upward_w[...], rep32)
    for row in range(4):
        block = jnp.where(lane64 // 64 == row, lifted, 0.0)
        w_upward[64 * row : 64 * row + 64, :] = block.astype(BF16)
    skipped = dot_tn(skip_w[...], rep32)
    for row in range(8):
        block = jnp.where(lane32 // 32 == row, skipped, 0.0)
        w_skip[32 * row : 32 * row + 32, :] = block.astype(BF16)
    row_id = lax.broadcasted_iota(jnp.int32, (64, 256), 0)
    for dc in range(3):
        taps = [dot(enter_w[p, dc], rep32) for p in range(3)]
        for variant in range(4):
            for channel in range(2):
                block = jnp.zeros((64, 256), F32)
                for p in range(3):
                    hit = row_id - 15 - 8 * variant - p == lane64 // 32
                    block = block + jnp.where(hit, taps[p][channel : channel + 1, :], 0.0)
                at = dc * 128 + channel * 64
                w_enter[variant, at : at + 64, :] = block.astype(BF16)
    for row, ref in enumerate(weights[8:]):
        biases[row : row + 1, :] = jnp.concatenate([ref[...]] * (256 // ref.shape[1]), axis=1)
    biases[6:8, :] = jnp.zeros((2, 256), F32)
    for k in (0, 6, 7, 8):
        saves[k].start()

    def store(y, value):
        image[pl.ds(8 + y, 32, stride=8), :] = value

    image[0:8] = jnp.zeros((8, 128), F32)
    image[264:272] = jnp.zeros((8, 128), F32)

    wait_bytes(landed3.at[pl.ds(0, 31)], recv_sem.at[2])
    row_transform(landed3[...].reshape(512, 128), third, twist2, fourth, store)
    whole = image[...].reshape(34, 8, 128)
    lane = lax.broadcasted_iota(jnp.int32, (32, 8, 128), 2)
    outer = jnp.where(lane < 64, whole[2:34], whole[0:32])
    downs[...] = jnp.concatenate([whole[1:33], outer], axis=1).astype(BF16)
    send_all("gx", NX, gx, downs, landed4, send_sem.at[3], recv_sem.at[3])

    def beside(other_y, slot):
        def one(x, carry):
            pltpu.make_async_remote_copy(
                src_ref=downs.at[x],
                dst_ref=sides.at[slot],
                send_sem=send_sem.at[8 + slot],
                recv_sem=recv_sem.at[8 + slot],
                device_id={"gx": x, "gy": other_y},
                device_id_type=MESH,
            ).start()
            return carry

        lax.fori_loop(0, NX, one, 0)

    @pl.when(gx == NX - 1)
    def _():
        beside(right_y, 0)

    @pl.when(gx == 0)
    def _():
        beside(left_y, 1)

    for copy in col_copies:
        copy.wait()
    save_rows.start()
    save_cols.start()

    wait_bytes(landed4.at[pl.ds(0, 31)], recv_sem.at[3])
    save_main.start()
    wait_bytes(sides.at[0], recv_sem.at[8])
    wait_bytes(sides.at[1], recv_sem.at[9])
    save_sides.start()
    for save in saves + [save_rows, save_cols]:
        save.wait()
    save_main.wait()
    save_sides.wait()
    wait_bytes(tiles.at[pl.ds(0, 15)], send_sem.at[0])
    wait_bytes(bands.at[pl.ds(0, 15)], send_sem.at[1])
    wait_bytes(ups.at[pl.ds(0, 31)], send_sem.at[2])
    wait_bytes(downs.at[pl.ds(0, 31)], send_sem.at[3])

    @pl.when(gx == NX - 1)
    def _():
        wait_bytes(downs, send_sem.at[8])

    @pl.when(gx == 0)
    def _():
        wait_bytes(downs, send_sem.at[9])


def exchange(vis, counts, owner, kernels, sky, weights):
    hbm = pl.BlockSpec(memory_space=pltpu.HBM)
    operands = transform_constants() + (kernels, vis, counts, owner, sky) + weights
    shapes = [
        (34, 16, 128),
        (2, 16, 256),
        (2, 160, 128),
        (4, 384, 256),
        (1024, 256),
        (1152, 256),
        (1152, 256),
        (1024, 256),
        (512, 256),
        (256, 256),
        (256, 256),
    ]
    outs = [jax.ShapeDtypeStruct(shape, BF16) for shape in shapes]
    outs.append(jax.ShapeDtypeStruct((8, 256), F32))
    return pl.pallas_call(
        exchange_kernel,
        out_shape=tuple(outs),
        in_specs=[hbm] * len(operands),
        out_specs=(hbm,) * len(outs),
        scratch_shapes=[pltpu.VMEM(x.shape, x.dtype) for x in list(operands) + outs[3:]]
        + [
            pltpu.VMEM((16, 16, 256), BF16),
            pltpu.VMEM((16, 16, 256), BF16),
            pltpu.VMEM((16, 32, 128), BF16),
            pltpu.VMEM((16, 32, 128), BF16),
            pltpu.VMEM((32, 16, 128), BF16),
            pltpu.VMEM((32, 16, 128), BF16),
            pltpu.VMEM((272, 128), F32),
            pltpu.VMEM((32, 16, 128), BF16),
            pltpu.VMEM((32, 16, 128), BF16),
            pltpu.VMEM((2, 16, 128), BF16),
            pltpu.VMEM((2, 16, 256), BF16),
            pltpu.VMEM((2, 160, 128), BF16),
            pltpu.VMEM((2, 160, 128), BF16),
            pltpu.VMEM((128, 256), BF16),
            pltpu.SemaphoreType.DMA((10,)),
            pltpu.SemaphoreType.DMA((10,)),
            pltpu.SemaphoreType.DMA((len(operands),)),
            pltpu.SemaphoreType.DMA((13,)),
        ],
        compiler_params=pltpu.CompilerParams(
            collective_id=0, has_side_effects=True, vmem_limit_bytes=64 << 20
        ),
        name="exchange",
    )(*operands)


def network_kernel(*refs):
    sources, (dirty_out, estimate_out), targets = refs[:16], refs[16:18], refs[18:34]
    window, entry, fine_a, fine_b, fine_c, pooled, coarse, mask, drawn, load_sem = refs[34:]
    loads = [
        pltpu.make_async_copy(source, target, load_sem.at[k])
        for k, (source, target) in enumerate(zip(sources, targets))
    ]
    for load in loads:
        load.start()
    sky, dirty_in, rows_in, cols_in, eye, into, w_enter, biases = targets[:8]
    w_encode, w_coarse, w_deeper, w_upward, w_skip, w_decode, w_output, back = targets[8:]

    def arrived(first, last):
        for load in loads[first:last]:
            load.wait()

    gx, gy = lax.axis_index("gx"), lax.axis_index("gy")
    last_x, last_y = lax.axis_size("gx") - 1, lax.axis_size("gy") - 1
    keep_top = jnp.where(gx == 0, 0.0, 1.0).astype(F32)
    keep_bottom = jnp.where(gx == last_x, 0.0, 1.0).astype(F32)

    slab = lax.broadcasted_iota(jnp.int32, (20, 16, 128), 0)
    stripe = lax.broadcasted_iota(jnp.int32, (20, 16, 128), 1)
    col = SLABS * stripe + slab - 9 + 256 * gy
    mask[...] = jnp.where((col >= 0) & (col < 256 * (last_y + 1)), 1.0, 0.0).astype(F32)

    arrived(0, 6)
    lane = lax.broadcasted_iota(jnp.int32, (160, 128), 1)
    beside = jnp.where(lane < 64, cols_in[1].astype(F32), cols_in[0].astype(F32))
    above = rows_in[0].astype(F32)[8:16] * keep_top
    below = rows_in[1].astype(F32)[0:8] * keep_bottom
    zeros = jnp.zeros((32, 256), F32)
    window[0, :, 0:256] = jnp.concatenate(
        [zeros[:16], above, sky[...], below, zeros], axis=0
    ).astype(BF16)
    beside = jnp.concatenate(
        [
            zeros[:16, :128],
            beside[8:16] * keep_top,
            beside[16:144],
            beside[144:152] * keep_bottom,
            zeros[:, :128],
        ],
        axis=0,
    )
    window[0, :, 256:384] = beside.astype(BF16)
    wide = dirty_in[...].astype(F32)
    gap = jnp.zeros((112, 128), F32)
    parts = []
    for half in range(2):
        rows8 = slice(8 * half, 8 * half + 8)
        stacked = jnp.concatenate(
            [wide[0:32, rows8].reshape(256, 128), wide[33, rows8], gap, wide[32, rows8]], axis=0
        )
        parts.append(dot_nt(eye[...], stacked.astype(BF16)))
    dirty_out[...] = parts[0][:, 0:256]
    zeros = jnp.zeros((32, 384), F32)
    window[1] = jnp.concatenate(
        [zeros[:16], parts[1][120:128] * keep_top, parts[0], parts[1][0:8] * keep_bottom, zeros],
        axis=0,
    ).astype(BF16)
    for q in range(5):
        rows64 = slice(32 * q, 32 * q + 64)
        both = jnp.concatenate([window[0, rows64], window[1, rows64]], axis=0)
        placed = dot_nt(into[...], both).reshape(20, 16, 128) * mask[...]
        entry[q] = placed.astype(BF16)

    blank = jnp.zeros((20, 16, 128), BF16)
    for ref, top in ((fine_a, 37), (fine_b, 37), (fine_c, 37), (pooled, 37), (coarse, 37)):
        ref[0] = blank[: ref.shape[1]]
        ref[top] = blank[: ref.shape[1]]

    def row_keep(group):
        top = jnp.where(group == 0, keep_top, 1.0)
        bottom = jnp.where(group == GROUPS - 1, keep_bottom, 1.0)
        return top * bottom

    def put(ref, at, value, slabs):
        ref[at, 1 : slabs + 1] = value.astype(BF16)
        ref[at, 0] = pltpu.roll(value[slabs - 1], 1, 0).astype(BF16)
        ref[at, slabs + 1] = pltpu.roll(value[0], STRIPES - 1, 0).astype(BF16)

    def finish(total, bias_row, keep):
        value = jnp.maximum(total + biases[bias_row : bias_row + 1, :], 0.0)
        scaled = mask[1:19] * keep
        return [
            value[:, 128 * h : 128 * h + 128].reshape(SLABS, 16, 128) * scaled for h in range(2)
        ]

    def beside(ref, group, slabs):
        lanes = lax.broadcasted_iota(jnp.int32, (slabs, 16, 128), 2)
        return jnp.where(lanes < 64, ref[2 * group + 3, 0:slabs], ref[2 * group, 0:slabs])

    def gathered(ref, first, count, slabs, pack):
        columns = [[] for _ in range(8 if pack else 9)]
        for group in range(count):
            group = first + group
            for dc in range(3):
                for h in range(2):
                    piece = ref[2 * group + 1 + h, dc : dc + slabs]
                    columns[2 * dc + h].append(piece.reshape(slabs * 16, 128))
            edge = beside(ref, group, slabs + 2)
            edges = [edge[dc : dc + slabs].reshape(slabs * 16, 128) for dc in range(3)]
            if pack:
                lanes = lax.broadcasted_iota(jnp.int32, (slabs * 16, 128), 1)
                turned = jnp.concatenate([edges[0][:, 64:], edges[0][:, :64]], axis=1)
                middle = (lanes >= 32) & (lanes < 96)
                edges = [jnp.where(middle, turned, edges[1]), edges[2]]
            for k, edge in enumerate(edges):
                columns[6 + k].append(edge)
        return jnp.concatenate([jnp.concatenate(c, axis=0) for c in columns], axis=1)

    arrived(6, 8)
    for variant in range(4):
        members = list(range(variant, GROUPS, 4))
        pieces = []
        for dc in range(3):
            rows = [entry[group // 4, dc : dc + SLABS].reshape(PIX, 128) for group in members]
            pieces.append(jnp.concatenate(rows, axis=0))
        total = dot(jnp.concatenate(pieces, axis=1), w_enter[variant])
        for g, group in enumerate(members):
            for h, value in enumerate(finish(total[PIX * g : PIX * g + PIX], 0, row_keep(group))):
                put(fine_a, 2 * group + 1 + h, value, SLABS)

    def encode_step(step, carry):
        total = dot(gathered(fine_a, GE * step, GE, SLABS, True), w_encode[...])
        for g in range(GE):
            group = GE * step + g
            for h, value in enumerate(finish(total[PIX * g : PIX * g + PIX], 1, row_keep(group))):
                put(fine_b, 2 * group + 1 + h, value, SLABS)
                pair = value.reshape(SLABS // 2, 2, 16, 128)
                put(pooled, 2 * group + 1 + h, (pair[:, 0] + pair[:, 1]) * 0.25, SLABS // 2)
        return carry

    arrived(8, 9)
    lax.fori_loop(0, GROUPS // GE, encode_step, 0)

    even_mask = mask[1:19].reshape(SLABS // 2, 2, 16, 128)[:, 0]

    def coarse_step(step, carry):
        total = dot(gathered(pooled, GC * step, GC, SLABS // 2, False), w_coarse[...])
        for g in range(GC):
            group = GC * step + g
            value = jnp.maximum(total[PIX2 * g : PIX2 * g + PIX2] + biases[2:3, :], 0.0)
            scaled = even_mask * row_keep(group)
            for h in range(2):
                half = value[:, 128 * h : 128 * h + 128].reshape(SLABS // 2, 16, 128) * scaled
                put(coarse, 2 * group + 1 + h, half, SLABS // 2)
        return carry

    arrived(9, 10)
    lax.fori_loop(0, GROUPS // GC, coarse_step, 0)

    def merge_step(step, carry):
        total = dot(gathered(coarse, GM * step, GM, SLABS // 2, False), w_deeper[...])
        value = jnp.maximum(total + biases[3:4, :], 0.0).astype(BF16)
        lifted = dot(value, w_upward[...]).reshape(GM, SLABS // 2, 1, 16, 256)
        halves = []
        for h in range(2):
            rows = [
                fine_b[2 * (GM * step + g) + 1 + h, 1:19].reshape(PIX, 128) for g in range(GM)
            ]
            halves.append(jnp.concatenate(rows, axis=0))
        skipped = dot(jnp.concatenate(halves, axis=1), w_skip[...])
        total = skipped.reshape(GM, SLABS // 2, 2, 16, 256) + lifted
        total = total.reshape(GM * PIX, 256)
        for g in range(GM):
            group = GM * step + g
            for h, half in enumerate(finish(total[PIX * g : PIX * g + PIX], 4, row_keep(group))):
                put(fine_a, 2 * group + 1 + h, half, SLABS)
        return carry

    arrived(10, 13)
    lax.fori_loop(0, GROUPS // GM, merge_step, 0)

    def decode_step(step, carry):
        total = dot(gathered(fine_a, GD * step, GD, SLABS, True), w_decode[...])
        for g in range(GD):
            group = GD * step + g
            for h, half in enumerate(finish(total[PIX * g : PIX * g + PIX], 5, row_keep(group))):
                put(fine_c, 2 * group + 1 + h, half, SLABS)
        return carry

    arrived(13, 14)
    lax.fori_loop(0, GROUPS // GD, decode_step, 0)

    lane_row = lax.broadcasted_iota(jnp.int32, (320, 256), 1) // 8 % 8

    def output_step(half, carry):
        columns = []
        for h in range(4):
            rows = [fine_c[2 * (8 * half + g + 1) + h].reshape(320, 128) for g in range(8)]
            columns.append(jnp.concatenate(rows, axis=0))
        total = dot(jnp.concatenate(columns, axis=1), w_output[...])
        kept = total[0:320]
        for g in range(1, 8):
            kept = jnp.where(lane_row == g, total[320 * g : 320 * g + 320], kept)
        drawn[half] = kept
        return carry

    arrived(14, 16)
    lax.fori_loop(0, 2, output_step, 0)

    sums = []
    for half in range(2):
        taps = drawn[half].reshape(20, 16, 256)
        left = taps[0:18, :, 0:128] + taps[2:20, :, 128:256]
        middle = taps[1:19, :, 0:128].reshape(PIX, 128)
        sums.append((left.reshape(PIX, 128), pltpu.roll(middle, 64, 1)))
    lanes = lax.broadcasted_iota(jnp.int32, (PIX, 128), 1)
    upper = sums[0][0] + sums[0][1]
    lower = pltpu.roll(sums[1][0] + sums[1][1], 64, 1)
    update = jnp.where(lanes < 64, upper, lower)
    high = update.astype(BF16)
    low = (update - high.astype(F32)).astype(BF16)
    ordered = dot(back[...], high) + dot(back[...], low)
    estimate_out[...] = sky[...] + ordered.T


def network(sky, dirty_in, rows_in, cols_in, bands):
    vmem, hbm = pl.BlockSpec(memory_space=pltpu.VMEM), pl.BlockSpec(memory_space=pltpu.HBM)
    into, back = permutations()
    eye = jnp.asarray(np.eye(128), BF16)
    enter, encode, coarse, deeper, decode, output, upward, skip, biases = bands
    operands = (sky, dirty_in, rows_in, cols_in, eye, into, enter, biases)
    operands += (encode, coarse, deeper, upward, skip, decode, output, back)
    return pl.pallas_call(
        network_kernel,
        out_shape=(
            jax.ShapeDtypeStruct((128, 256), F32),
            jax.ShapeDtypeStruct((128, 256), F32),
        ),
        in_specs=[hbm] * len(operands),
        out_specs=(vmem, vmem),
        scratch_shapes=[pltpu.VMEM(x.shape, x.dtype) for x in operands]
        + [
            pltpu.VMEM((2, 192, 384), BF16),
            pltpu.VMEM((5, 20, 16, 128), BF16),
            pltpu.VMEM((38, 20, 16, 128), BF16),
            pltpu.VMEM((38, 20, 16, 128), BF16),
            pltpu.VMEM((38, 20, 16, 128), BF16),
            pltpu.VMEM((38, 11, 16, 128), BF16),
            pltpu.VMEM((38, 11, 16, 128), BF16),
            pltpu.VMEM((20, 16, 128), F32),
            pltpu.VMEM((2, 320, 256), F32),
            pltpu.SemaphoreType.DMA((len(operands),)),
        ],
        compiler_params=pltpu.CompilerParams(vmem_limit_bytes=64 << 20),
        name="network",
    )(*operands)


def raw_weights(ew, eb, nw, nb, cw, cb, dw, db, uw, sw, mb, ow, ob, fw):
    biases = tuple(b.reshape(1, -1) for b in (eb, nb, cb, db, mb, ob))
    return (
        jnp.swapaxes(ew, 2, 3),
        nw,
        jnp.swapaxes(cw, 2, 3),
        dw,
        ow,
        fw[:, :, 0, :],
        uw,
        sw,
    ) + biases


def shards(
    sky_image,
    visibilities,
    grid_kernels,
    tile_counts,
    block_tiles,
    *parameters,
):
    slots = block_tiles.shape[2]
    dirty, rows, cols, *bands = exchange(
        visibilities[0, 0],
        tile_counts.reshape(1, -1),
        block_tiles.reshape(1, -1),
        grid_kernels.reshape(slots * 64, 256),
        sky_image,
        raw_weights(*parameters),
    )
    return network(sky_image, dirty, rows, cols, tuple(bands))


def solution(mesh):
    block = P("gx", "gy")
    return jax.shard_map(
        shards,
        mesh=mesh,
        in_specs=(
            block,
            P("gx", "gy", None, None, None),
            P("gx", "gy", None, None, None),
            P("gx", "gy", None),
            P("gx", "gy", None),
        )
        + (P(),) * 14,
        out_specs=(block, block),
        check_vma=False,
    )
```

```python
import functools
import math

import jax
import jax.numpy as jnp
import numpy as np
from jax import lax
from jax.experimental import pallas as pl
from jax.experimental.pallas import tpu as pltpu
from jax.sharding import PartitionSpec as P

MESH = pl.DeviceIdType.MESH
F32 = jnp.float32
BF16 = jnp.bfloat16

GE, GC, GM, GN, GD = 9, 9, 9, 9, 9
NX, NY = 32, 16
SLABS = 18
STRIPES = 16
PIX = SLABS * STRIPES
PIX2 = PIX // 2
GROUPS = 18


def dot(a, b):
    return jnp.dot(a, b, preferred_element_type=F32)


def dot_nt(a, b):
    return lax.dot_general(a, b, (((1,), (1,)), ((), ())), preferred_element_type=F32)


def complex_block(c, s):
    return np.stack([np.stack([c, -s]), np.stack([s, c])])


def transform_constants():
    turn = 2.0 * math.pi
    y0 = np.arange(128)
    cells = np.arange(256)
    ang = turn * (np.outer(y0, y0) % 128) / 128
    first = complex_block(np.cos(ang), np.sin(ang))
    first = first.reshape(2, 2, 128, 16, 8).transpose(0, 2, 3, 1, 4).reshape(256, 256)
    ang = turn * np.outer(y0, cells % 32) / 4096
    sign = np.where(y0 % 2 == 0, 1.0, -1.0)[:, None]
    twist1 = np.stack([np.cos(ang) * sign, np.sin(ang) * sign])
    short = np.arange(32)
    ang = turn * (np.outer(short, short) % 32) / 32
    c32, s32 = np.cos(ang), np.sin(ang)
    second = complex_block(c32, s32)
    second = np.einsum("abys,rt->yarbts", second, np.eye(8)).reshape(512, 512)
    third = complex_block(c32, s32)
    third = np.einsum("abxi,yz->ayxibz", third, np.eye(8)).reshape(512, 512)
    ang = turn * np.outer(y0, y0) / 4096
    twist2 = np.stack([np.cos(ang) * sign, np.sin(ang) * sign]) / 4096
    ang = turn * (np.outer(short, y0) % 32) / 32
    fourth = np.concatenate([np.cos(ang), -np.sin(ang)], axis=1)
    return (
        jnp.asarray(first, BF16),
        jnp.asarray(twist1, F32),
        jnp.asarray(second, BF16),
        jnp.asarray(third, BF16),
        jnp.asarray(twist2, F32),
        jnp.asarray(fourth, BF16),
        jnp.asarray(np.eye(128), BF16),
    )


def permutations():
    into = np.zeros((20, STRIPES, 384), np.float32)
    back = np.zeros((256, SLABS, STRIPES), np.float32)
    for w in range(-1, SLABS + 1):
        for s in range(STRIPES):
            col = SLABS * s + w - 8
            if 0 <= col < 264:
                into[w + 1, s, col] = 1
            elif -8 <= col < 0:
                into[w + 1, s, 384 + col] = 1
            if 0 <= col < 256 and 0 <= w < SLABS:
                back[col, w, s] = 1
    return jnp.asarray(into.reshape(320, 384), BF16), jnp.asarray(back.reshape(256, PIX), BF16)


def farthest_first(step, count, me):
    away = (step + 1) // 2
    shift = count // 2 + jnp.where(step % 2 == 1, away, -away)
    return lax.rem(me + shift, count)


def send_all(axis, count, me, source, landing, send_sem, recv_sem):
    def one(step, carry):
        other = farthest_first(step, count, me)
        pltpu.make_async_remote_copy(
            src_ref=source.at[other],
            dst_ref=landing.at[me],
            send_sem=send_sem,
            recv_sem=recv_sem,
            device_id={axis: other},
            device_id_type=MESH,
        ).start()
        return carry

    lax.fori_loop(0, count - 1, one, 0)
    landing[me] = source[me]


def wait_bytes(ref, sem):
    pltpu.make_async_copy(ref, ref, sem).wait()


def grid_tiles(vis, counts, owner, kernels):
    wide = vis[...].astype(F32)
    parts = [jnp.concatenate([wide[:, k, :]] * 2, axis=1) for k in range(2)]
    slot = lax.broadcasted_iota(jnp.int32, (64, 128), 0)
    half = lax.broadcasted_iota(jnp.int32, (64, 128), 1) // 64
    contrib = None
    for piece in range(8):
        blocks = []
        for q in range(4 * piece, 4 * piece + 4):
            hit = slot == 2 * q + half
            block = [jnp.where(hit, part, 0.0).astype(BF16) for part in parts]
            blocks.append(jnp.concatenate(block, axis=0))
        term = dot(jnp.concatenate(blocks, axis=1), kernels[512 * piece : 512 * piece + 512, :])
        contrib = term if contrib is None else contrib + term
    live = jnp.sum(counts[...], axis=1, keepdims=True)
    both = jnp.concatenate([owner[...]] * 2, axis=1)
    lane = lax.broadcasted_iota(jnp.int32, (1, 128), 1) % 64
    both = jnp.where(lane < live, both, -1)
    chosen = jnp.where(lax.broadcasted_iota(jnp.int32, (128, 128), 0) == both, 1.0, 0.0)
    chosen = chosen.astype(BF16)
    sums = []
    for k in range(2):
        own = contrib[64 * k : 64 * k + 64]
        high = own.astype(BF16)
        low = (own - high.astype(F32)).astype(BF16)
        total = dot(chosen, jnp.concatenate([high, low], axis=0))
        sums.append(total.reshape(16, 8, 256))
    return jnp.concatenate(sums, axis=1).astype(BF16)


def column_transform(held, first, twist1, second):
    turned = dot(first[...], held)
    real, imag = turned[:128], turned[128:]
    c, s = twist1[0], twist1[1]
    both = jnp.concatenate([real * c - imag * s, real * s + imag * c], axis=1).astype(BF16)
    return dot_nt(second[...], both)


def columns_up(held, eye):
    wide = held.astype(F32).reshape(16, 4, 8, 128)
    halves = []
    for y1 in range(2):
        parts = []
        for part in range(2):
            piece = wide[:, 2 * y1 + part].reshape(128, 128).astype(BF16)
            parts.append(dot_nt(eye, piece).reshape(16, 8, 128))
        halves.append(jnp.concatenate(parts, axis=1))
    return jnp.concatenate(halves, axis=0).astype(BF16)


def row_transform(held, third, twist2, fourth, store):
    turned = dot(third[...], held)
    for y in range(8):
        real = turned[32 * y : 32 * y + 32]
        imag = turned[256 + 32 * y : 256 + 32 * y + 32]
        real = jnp.concatenate([real] * 4, axis=0)
        imag = jnp.concatenate([imag] * 4, axis=0)
        c, s = twist2[0], twist2[1]
        both = jnp.concatenate([real * c - imag * s, real * s + imag * c], axis=1).astype(BF16)
        store(y, dot_nt(fourth[...], both))


def repeat_matrix(rows):
    row = lax.broadcasted_iota(jnp.int32, (rows, 256), 0)
    lane = lax.broadcasted_iota(jnp.int32, (rows, 256), 1)
    return jnp.where(lane % rows == row, 1.0, 0.0).astype(BF16)


def dot_tn(a, b):
    return lax.dot_general(a, b, (((0,), (0,)), ((), ())), preferred_element_type=F32)


def band(dst, tile, high, rows, out_row, place, lane_id, count):
    for dc in range(3):
        taps = [tile(p, dc) for p in range(3)]
        for row in rows:
            block = jnp.zeros(lane_id.shape, F32)
            for p in range(3):
                if 0 <= out_row(row, p) < count:
                    block = block + jnp.where(lane_id == out_row(row, p), taps[p], 0.0)
            at = place(dc, row)
            dst[at : at + high, :] = block.astype(BF16)


def place_fine(dc, row):
    if row == 3:
        return (800, 864, 992)[dc]
    if row == 12:
        return (832, 768, 896)[dc]
    return 256 * dc + 32 * (row - 4)


def place_coarse(dc, row):
    if row < 4:
        return 768 + 128 * dc + 64 + 32 * (row - 2)
    if row > 11:
        return 768 + 128 * dc + 32 * (row - 12)
    return 256 * dc + 32 * (row - 4)


def place_deeper(dc, row):
    if row == 1:
        return 768 + 128 * dc + 64
    if row == 6:
        return 768 + 128 * dc
    return 256 * dc + 64 * (row - 2)


def exchange_kernel(*refs):
    (
        first_h,
        twist1_h,
        second_h,
        third_h,
        twist2_h,
        fourth_h,
        eye_h,
        kernels_h,
        vis_h,
        counts_h,
        owner_h,
        sky_h,
    ) = refs[:12]
    weights_h = refs[12:26]
    dirty_out, rows_out, cols_out = refs[26:29]
    bands_out = refs[29:37]
    (
        first,
        twist1,
        second,
        third,
        twist2,
        fourth,
        eye,
        kernels,
        vis,
        counts,
        owner,
        sky,
    ) = refs[37:49]
    weights = refs[49:63]
    built = refs[63:71]
    w_enter, w_encode, w_coarse, w_deeper, w_decode, w_output, w_merge, biases = built
    (
        tiles,
        landed1,
        bands,
        landed2,
        ups,
        landed3,
        image,
        downs,
        landed4,
        sides,
        sky_rows,
        sky_sides,
        sky_cols,
        sky_own,
        send_sem,
        recv_sem,
        load_sem,
        save_sem,
    ) = refs[71:]
    saves = [
        pltpu.make_async_copy(source, target, save_sem.at[k])
        for k, (source, target) in enumerate(zip(built, bands_out))
    ]
    save_rows = pltpu.make_async_copy(sky_rows, rows_out, save_sem.at[8])
    save_cols = pltpu.make_async_copy(sky_sides, cols_out, save_sem.at[9])
    save_main = pltpu.make_async_copy(landed4, dirty_out.at[pl.ds(0, 32)], save_sem.at[10])
    save_sides = pltpu.make_async_copy(sides, dirty_out.at[pl.ds(32, 2)], save_sem.at[11])
    gx, gy = lax.axis_index("gx"), lax.axis_index("gy")
    down_x, up_x = lax.rem(gx + 1, NX), lax.rem(gx + NX - 1, NX)
    right_y, left_y = lax.rem(gy + 1, NY), lax.rem(gy + NY - 1, NY)
    barrier = pltpu.get_barrier_semaphore()

    def greet(axis, count, me):
        def one(step, carry):
            other = farthest_first(step, count, me)
            pl.semaphore_signal(barrier, inc=1, device_id={axis: other}, device_id_type=MESH)
            return carry

        lax.fori_loop(0, count - 1, one, 0)

    greet("gy", NY, gy)
    greet("gx", NX, gx)
    for x, y in ((NX - 1, left_y), (0, right_y)):
        pl.semaphore_signal(barrier, inc=1, device_id={"gx": x, "gy": y}, device_id_type=MESH)

    sources = (kernels_h, vis_h, counts_h, owner_h, sky_h, first_h, twist1_h, second_h)
    sources += weights_h + (third_h, twist2_h, fourth_h, eye_h)
    targets = (kernels, vis, counts, owner, sky, first, twist1, second)
    targets += weights + (third, twist2, fourth, eye)
    loads = [
        pltpu.make_async_copy(source, target, load_sem.at[k])
        for k, (source, target) in enumerate(zip(sources, targets))
    ]
    for load in loads:
        load.start()

    for load in loads[:5]:
        load.wait()
    sky_own[...] = sky[...].astype(BF16)
    tiles[...] = grid_tiles(vis, counts, owner, kernels)
    edge = jnp.where((gx == 0) | (gx == NX - 1), NX, 0)
    pl.semaphore_wait(barrier, NX + NY - 2 + edge)

    send_all("gy", NY, gy, tiles, landed1, send_sem.at[0], recv_sem.at[0])

    def to_side(source, target, slot, axis, other):
        return pltpu.make_async_remote_copy(
            src_ref=source,
            dst_ref=target,
            send_sem=send_sem.at[slot],
            recv_sem=recv_sem.at[slot],
            device_id={axis: other},
            device_id_type=MESH,
        )

    row_copies = [
        to_side(sky_own.at[pl.ds(112, 16)], sky_rows.at[0], 4, "gx", down_x),
        to_side(sky_own.at[pl.ds(0, 16)], sky_rows.at[1], 5, "gx", up_x),
    ]
    for copy in row_copies:
        copy.start()

    for load in loads[5:]:
        load.wait()
    enter_w, encode_w, coarse_w, deeper_w, decode_w, output_w, upward_w, skip_w = weights[:8]
    rep32, rep64 = repeat_matrix(32), repeat_matrix(64)
    lane32 = lax.broadcasted_iota(jnp.int32, (32, 256), 1)
    lane64 = lax.broadcasted_iota(jnp.int32, (64, 256), 1)
    rows = range(3, 13)

    def fine_row(row, p):
        return row - 3 - p

    for dst, raw, save in ((w_encode, encode_w, saves[1]), (w_decode, decode_w, saves[4])):
        dst[928:992, :] = jnp.zeros((64, 256), BF16)

        def tile(p, dc, raw=raw):
            return dot_tn(raw[p, dc], rep32)

        band(dst, tile, 32, rows, fine_row, place_fine, lane32 // 32, 8)
        save.start()

    wait_bytes(landed1.at[pl.ds(0, 15)], recv_sem.at[0])
    turned = column_transform(landed1[...].reshape(256, 256), first, twist1, second)
    bands[...] = turned.astype(BF16).reshape(16, 32, 128)
    send_all("gy", NY, gy, bands, landed2, send_sem.at[1], recv_sem.at[1])

    for copy in row_copies:
        copy.wait()
    above, below = sky_rows[0].astype(F32)[8:16], sky_rows[1].astype(F32)[0:8]
    outer_rows = jnp.concatenate([below, jnp.zeros((112, 256), F32), above], axis=0).astype(BF16)
    for half, chosen, at in ((0, eye[0:16], 0), (1, eye[112:128], 8)):
        lanes = slice(128 * half, 128 * half + 128)
        both = [dot_nt(chosen, sky_own[:, lanes]), dot_nt(chosen, outer_rows[:, lanes])]
        both = [part[at : at + 8] for part in both]
        sky_cols[half] = jnp.concatenate(both, axis=0).astype(BF16)
    col_copies = [
        to_side(sky_cols.at[1], sky_sides.at[0], 6, "gy", right_y),
        to_side(sky_cols.at[0], sky_sides.at[1], 7, "gy", left_y),
    ]
    for copy in col_copies:
        copy.start()

    def coarse_tile(p, dc):
        return dot(coarse_w[p, dc], rep64)

    def coarse_row(row, p):
        return row // 2 - 1 - p

    band(w_coarse, coarse_tile, 32, range(2, 14), coarse_row, place_coarse, lane32 // 64, 4)
    saves[2].start()

    def deeper_tile(p, dc):
        return dot_tn(deeper_w[p, dc], rep64)

    def deeper_row(row, p):
        return row - 1 - p

    band(w_deeper, deeper_tile, 64, range(1, 7), deeper_row, place_deeper, lane64 // 64, 4)
    saves[3].start()
    tap_row = lax.broadcasted_iota(jnp.int32, (3, 256), 0)
    tap_lane = lax.broadcasted_iota(jnp.int32, (3, 256), 1) // 64
    own = jnp.where(tap_row == tap_lane, 1.0, 0.0).astype(BF16)
    taps = [dot_tn(output_w[p], own) for p in range(3)]
    for row in range(16):
        block = jnp.zeros((32, 256), F32)
        for p in range(3):
            if 0 <= row - 3 - p < 8:
                block = block + jnp.where(lane32 % 8 == row - 3 - p, taps[p], 0.0)
        w_output[32 * row : 32 * row + 32, :] = block.astype(BF16)
    saves[5].start()

    wait_bytes(landed2.at[pl.ds(0, 15)], recv_sem.at[1])
    ups[...] = columns_up(landed2[...], eye[...])
    send_all("gx", NX, gx, ups, landed3, send_sem.at[2], recv_sem.at[2])

    lifted = dot_tn(upward_w[...], rep32)
    for row in range(4):
        block = jnp.where(lane64 // 64 == row, lifted, 0.0)
        w_merge[256 + 64 * row : 320 + 64 * row, :] = block.astype(BF16)
    skipped = dot_tn(skip_w[...], rep32)
    for row in range(8):
        block = jnp.where(lane32 // 32 == row, skipped, 0.0)
        w_merge[32 * row : 32 * row + 32, :] = block.astype(BF16)
    row_id = lax.broadcasted_iota(jnp.int32, (64, 256), 0)
    for dc in range(3):
        taps = [dot(enter_w[p, dc], rep32) for p in range(3)]
        for variant in range(4):
            for channel in range(2):
                block = jnp.zeros((64, 256), F32)
                for p in range(3):
                    hit = row_id - 15 - 8 * variant - p == lane64 // 32
                    block = block + jnp.where(hit, taps[p][channel : channel + 1, :], 0.0)
                at = dc * 128 + channel * 64
                w_enter[variant, at : at + 64, :] = block.astype(BF16)
    for row, ref in enumerate(weights[8:]):
        biases[row : row + 1, :] = jnp.concatenate([ref[...]] * (256 // ref.shape[1]), axis=1)
    biases[6:8, :] = jnp.zeros((2, 256), F32)
    for k in (0, 6, 7):
        saves[k].start()

    def store(y, value):
        image[pl.ds(8 + y, 32, stride=8), :] = value

    image[0:8] = jnp.zeros((8, 128), F32)
    image[264:272] = jnp.zeros((8, 128), F32)

    wait_bytes(landed3.at[pl.ds(0, 31)], recv_sem.at[2])
    row_transform(landed3[...].reshape(512, 128), third, twist2, fourth, store)
    whole = image[...].reshape(34, 8, 128)
    lane = lax.broadcasted_iota(jnp.int32, (32, 8, 128), 2)
    outer = jnp.where(lane < 64, whole[2:34], whole[0:32])
    downs[...] = jnp.concatenate([whole[1:33], outer], axis=1).astype(BF16)
    send_all("gx", NX, gx, downs, landed4, send_sem.at[3], recv_sem.at[3])

    def beside(other_y, slot):
        def one(x, carry):
            pltpu.make_async_remote_copy(
                src_ref=downs.at[x],
                dst_ref=sides.at[slot],
                send_sem=send_sem.at[8 + slot],
                recv_sem=recv_sem.at[8 + slot],
                device_id={"gx": x, "gy": other_y},
                device_id_type=MESH,
            ).start()
            return carry

        lax.fori_loop(0, NX, one, 0)

    @pl.when(gx == NX - 1)
    def _():
        beside(right_y, 0)

    @pl.when(gx == 0)
    def _():
        beside(left_y, 1)

    for copy in col_copies:
        copy.wait()
    save_rows.start()
    save_cols.start()

    wait_bytes(landed4.at[pl.ds(0, 31)], recv_sem.at[3])
    save_main.start()
    wait_bytes(sides.at[0], recv_sem.at[8])
    wait_bytes(sides.at[1], recv_sem.at[9])
    save_sides.start()
    for save in saves + [save_rows, save_cols]:
        save.wait()
    save_main.wait()
    save_sides.wait()
    wait_bytes(tiles.at[pl.ds(0, 15)], send_sem.at[0])
    wait_bytes(bands.at[pl.ds(0, 15)], send_sem.at[1])
    wait_bytes(ups.at[pl.ds(0, 31)], send_sem.at[2])
    wait_bytes(downs.at[pl.ds(0, 31)], send_sem.at[3])

    @pl.when(gx == NX - 1)
    def _():
        wait_bytes(downs, send_sem.at[8])

    @pl.when(gx == 0)
    def _():
        wait_bytes(downs, send_sem.at[9])


def exchange(vis, counts, owner, kernels, sky, weights):
    hbm = pl.BlockSpec(memory_space=pltpu.HBM)
    operands = transform_constants() + (kernels, vis, counts, owner, sky) + weights
    shapes = [
        (34, 16, 128),
        (2, 16, 256),
        (2, 16, 128),
        (4, 384, 256),
        (1024, 256),
        (1152, 256),
        (1152, 256),
        (1024, 256),
        (512, 256),
        (512, 256),
    ]
    outs = [jax.ShapeDtypeStruct(shape, BF16) for shape in shapes]
    outs.append(jax.ShapeDtypeStruct((8, 256), F32))
    return pl.pallas_call(
        exchange_kernel,
        out_shape=tuple(outs),
        in_specs=[hbm] * len(operands),
        out_specs=(hbm,) * len(outs),
        scratch_shapes=[pltpu.VMEM(x.shape, x.dtype) for x in list(operands) + outs[3:]]
        + [
            pltpu.VMEM((16, 16, 256), BF16),
            pltpu.VMEM((16, 16, 256), BF16),
            pltpu.VMEM((16, 32, 128), BF16),
            pltpu.VMEM((16, 32, 128), BF16),
            pltpu.VMEM((32, 16, 128), BF16),
            pltpu.VMEM((32, 16, 128), BF16),
            pltpu.VMEM((272, 128), F32),
            pltpu.VMEM((32, 16, 128), BF16),
            pltpu.VMEM((32, 16, 128), BF16),
            pltpu.VMEM((2, 16, 128), BF16),
            pltpu.VMEM((2, 16, 256), BF16),
            pltpu.VMEM((2, 16, 128), BF16),
            pltpu.VMEM((2, 16, 128), BF16),
            pltpu.VMEM((128, 256), BF16),
            pltpu.SemaphoreType.DMA((10,)),
            pltpu.SemaphoreType.DMA((10,)),
            pltpu.SemaphoreType.DMA((len(operands),)),
            pltpu.SemaphoreType.DMA((12,)),
        ],
        compiler_params=pltpu.CompilerParams(
            collective_id=0, has_side_effects=True, vmem_limit_bytes=64 << 20
        ),
        name="exchange",
    )(*operands)


def network_kernel(*refs):
    sources, (dirty_hbm, estimate_out), targets = refs[:15], refs[15:17], refs[17:32]
    window, entry, fine_a, fine_b, fine_c, pooled, coarse, deep, mask, drawn, dirty_out, load_sem = refs[32:]
    save_dirty = pltpu.make_async_copy(dirty_out, dirty_hbm, load_sem.at[15])
    loads = [
        pltpu.make_async_copy(source, target, load_sem.at[k])
        for k, (source, target) in enumerate(zip(sources, targets))
    ]
    for load in loads:
        load.start()
    sky, dirty_in, rows_in, cols_in, eye, into, w_enter, biases = targets[:8]
    w_encode, w_coarse, w_deeper, w_merge, w_decode, w_output, back = targets[8:]

    def arrived(first, last):
        for load in loads[first:last]:
            load.wait()

    gx, gy = lax.axis_index("gx"), lax.axis_index("gy")
    last_x, last_y = lax.axis_size("gx") - 1, lax.axis_size("gy") - 1
    keep_top = jnp.where(gx == 0, 0.0, 1.0).astype(F32)
    keep_bottom = jnp.where(gx == last_x, 0.0, 1.0).astype(F32)

    slab = lax.broadcasted_iota(jnp.int32, (20, 16, 128), 0)
    stripe = lax.broadcasted_iota(jnp.int32, (20, 16, 128), 1)
    col = SLABS * stripe + slab - 9 + 256 * gy
    mask[...] = jnp.where((col >= 0) & (col < 256 * (last_y + 1)), 1.0, 0.0).astype(F32)

    arrived(0, 6)
    above = rows_in[0].astype(F32)[8:16] * keep_top
    below = rows_in[1].astype(F32)[0:8] * keep_bottom
    zeros = jnp.zeros((32, 512), F32)
    window[0, :, 0:256] = jnp.concatenate(
        [zeros[:16, :256], above, sky[...], below, zeros[:, :256]], axis=0
    ).astype(BF16)
    wide, sides = dirty_in[...].astype(F32), cols_in[...].astype(F32)
    gap = jnp.zeros((112, 128), F32)
    parts = []
    for half in range(2):
        rows8 = slice(8 * half, 8 * half + 8)
        stacked = [wide[0:32, rows8].reshape(256, 128), wide[33, rows8], gap, wide[32, rows8]]
        stacked += [sides[1, rows8], gap, sides[0, rows8]]
        parts.append(dot_nt(eye[...], jnp.concatenate(stacked, axis=0).astype(BF16)))
    dirty_out[...] = parts[0][:, 0:256]
    save_dirty.start()
    whole = jnp.concatenate(
        [zeros[:16], parts[1][120:128] * keep_top, parts[0], parts[1][0:8] * keep_bottom, zeros],
        axis=0,
    ).astype(BF16)
    window[1] = whole[:, 0:384]
    window[0, :, 256:384] = whole[:, 384:512]
    pieces = []
    for q in range(5):
        rows64 = slice(32 * q, 32 * q + 64)
        pieces += [window[0, rows64], window[1, rows64]]
    placed = dot_nt(into[...], jnp.concatenate(pieces, axis=0))
    for q in range(5):
        value = placed[:, 128 * q : 128 * q + 128].reshape(20, 16, 128) * mask[...]
        entry[q] = value.astype(BF16)

    blank = jnp.zeros((20, 16, 128), BF16)
    for ref, top in ((fine_a, 37), (fine_b, 37), (fine_c, 37), (pooled, 37), (coarse, 37)):
        ref[0] = blank[: ref.shape[1]]
        ref[top] = blank[: ref.shape[1]]

    def row_keep(group):
        top = jnp.where(group == 0, keep_top, 1.0)
        bottom = jnp.where(group == GROUPS - 1, keep_bottom, 1.0)
        return top * bottom

    def put(ref, at, value, slabs):
        ref[at, 1 : slabs + 1] = value.astype(BF16)
        ref[at, 0] = pltpu.roll(value[slabs - 1], 1, 0).astype(BF16)
        ref[at, slabs + 1] = pltpu.roll(value[0], STRIPES - 1, 0).astype(BF16)

    def finish(total, bias_row, keep):
        value = jnp.maximum(total + biases[bias_row : bias_row + 1, :], 0.0)
        scaled = mask[1:19] * keep
        return [
            value[:, 128 * h : 128 * h + 128].reshape(SLABS, 16, 128) * scaled for h in range(2)
        ]

    def beside(ref, group, slabs):
        lanes = lax.broadcasted_iota(jnp.int32, (slabs, 16, 128), 2)
        return jnp.where(lanes < 64, ref[2 * group + 3, 0:slabs], ref[2 * group, 0:slabs])

    def gathered(ref, first, count, slabs, pack):
        columns = [[] for _ in range(8 if pack else 9)]
        for group in range(count):
            group = first + group
            for dc in range(3):
                for h in range(2):
                    piece = ref[2 * group + 1 + h, dc : dc + slabs]
                    columns[2 * dc + h].append(piece.reshape(slabs * 16, 128))
            edge = beside(ref, group, slabs + 2)
            edges = [edge[dc : dc + slabs].reshape(slabs * 16, 128) for dc in range(3)]
            if pack:
                lanes = lax.broadcasted_iota(jnp.int32, (slabs * 16, 128), 1)
                turned = jnp.concatenate([edges[0][:, 64:], edges[0][:, :64]], axis=1)
                middle = (lanes >= 32) & (lanes < 96)
                edges = [jnp.where(middle, turned, edges[1]), edges[2]]
            for k, edge in enumerate(edges):
                columns[6 + k].append(edge)
        return jnp.concatenate([jnp.concatenate(c, axis=0) for c in columns], axis=1)

    arrived(6, 8)
    for variant in range(4):
        members = list(range(variant, GROUPS, 4))
        pieces = []
        for dc in range(3):
            rows = [entry[group // 4, dc : dc + SLABS].reshape(PIX, 128) for group in members]
            pieces.append(jnp.concatenate(rows, axis=0))
        total = dot(jnp.concatenate(pieces, axis=1), w_enter[variant])
        for g, group in enumerate(members):
            for h, value in enumerate(finish(total[PIX * g : PIX * g + PIX], 0, row_keep(group))):
                put(fine_a, 2 * group + 1 + h, value, SLABS)

    def encode_step(step, carry):
        total = dot(gathered(fine_a, GE * step, GE, SLABS, True), w_encode[...])
        for g in range(GE):
            group = GE * step + g
            for h, value in enumerate(finish(total[PIX * g : PIX * g + PIX], 1, row_keep(group))):
                put(fine_b, 2 * group + 1 + h, value, SLABS)
                pair = value.reshape(SLABS // 2, 2, 16, 128)
                put(pooled, 2 * group + 1 + h, (pair[:, 0] + pair[:, 1]) * 0.25, SLABS // 2)
        return carry

    arrived(8, 9)
    lax.fori_loop(0, GROUPS // GE, encode_step, 0)

    even_mask = mask[1:19].reshape(SLABS // 2, 2, 16, 128)[:, 0]

    def coarse_step(step, carry):
        total = dot(gathered(pooled, GC * step, GC, SLABS // 2, False), w_coarse[...])
        for g in range(GC):
            group = GC * step + g
            value = jnp.maximum(total[PIX2 * g : PIX2 * g + PIX2] + biases[2:3, :], 0.0)
            scaled = even_mask * row_keep(group)
            for h in range(2):
                half = value[:, 128 * h : 128 * h + 128].reshape(SLABS // 2, 16, 128) * scaled
                put(coarse, 2 * group + 1 + h, half, SLABS // 2)
        return carry

    arrived(9, 10)
    lax.fori_loop(0, GROUPS // GC, coarse_step, 0)

    def deeper_step(step, carry):
        total = dot(gathered(coarse, GM * step, GM, SLABS // 2, False), w_deeper[...])
        value = jnp.maximum(total + biases[3:4, :], 0.0).astype(BF16)
        for g in range(GM):
            piece = value[PIX2 * g : PIX2 * g + PIX2].reshape(SLABS // 2, 16, 256)
            for h in range(2):
                deep[2 * (GM * step + g) + h] = piece[:, :, 128 * h : 128 * h + 128]
        return carry

    arrived(10, 11)
    lax.fori_loop(0, GROUPS // GM, deeper_step, 0)

    def merge_step(step, carry):
        columns = []
        for h in range(2):
            rows = [
                fine_b[2 * (GN * step + g) + 1 + h, 1:19].reshape(PIX, 128) for g in range(GN)
            ]
            columns.append(jnp.concatenate(rows, axis=0))
        for h in range(2):
            rows = []
            for g in range(GN):
                low = deep[2 * (GN * step + g) + h].reshape(SLABS // 2, 1, 16, 128)
                low = jnp.broadcast_to(low, (SLABS // 2, 2, 16, 128))
                rows.append(low.reshape(PIX, 128))
            columns.append(jnp.concatenate(rows, axis=0))
        total = dot(jnp.concatenate(columns, axis=1), w_merge[...])
        for g in range(GN):
            group = GN * step + g
            for h, half in enumerate(finish(total[PIX * g : PIX * g + PIX], 4, row_keep(group))):
                put(fine_a, 2 * group + 1 + h, half, SLABS)
        return carry

    arrived(11, 12)
    lax.fori_loop(0, GROUPS // GN, merge_step, 0)

    def decode_step(step, carry):
        total = dot(gathered(fine_a, GD * step, GD, SLABS, True), w_decode[...])
        for g in range(GD):
            group = GD * step + g
            for h, half in enumerate(finish(total[PIX * g : PIX * g + PIX], 5, row_keep(group))):
                put(fine_c, 2 * group + 1 + h, half, SLABS)
        return carry

    arrived(12, 13)
    lax.fori_loop(0, GROUPS // GD, decode_step, 0)

    lane_row = lax.broadcasted_iota(jnp.int32, (320, 256), 1) // 8 % 8

    def output_step(half, carry):
        columns = []
        for h in range(4):
            rows = [fine_c[2 * (8 * half + g + 1) + h].reshape(320, 128) for g in range(8)]
            columns.append(jnp.concatenate(rows, axis=0))
        total = dot(jnp.concatenate(columns, axis=1), w_output[...])
        kept = total[0:320]
        for g in range(1, 8):
            kept = jnp.where(lane_row == g, total[320 * g : 320 * g + 320], kept)
        drawn[half] = kept
        return carry

    arrived(13, 15)
    lax.fori_loop(0, 2, output_step, 0)

    sums = []
    for half in range(2):
        taps = drawn[half].reshape(20, 16, 256)
        left = taps[0:18, :, 0:128] + taps[2:20, :, 128:256]
        middle = taps[1:19, :, 0:128].reshape(PIX, 128)
        sums.append((left.reshape(PIX, 128), pltpu.roll(middle, 64, 1)))
    lanes = lax.broadcasted_iota(jnp.int32, (PIX, 128), 1)
    upper = sums[0][0] + sums[0][1]
    lower = pltpu.roll(sums[1][0] + sums[1][1], 64, 1)
    update = jnp.where(lanes < 64, upper, lower)
    high = update.astype(BF16)
    low = (update - high.astype(F32)).astype(BF16)
    ordered = dot(back[...], high) + dot(back[...], low)
    estimate_out[...] = sky[...] + ordered.T
    save_dirty.wait()


def network(sky, dirty_in, rows_in, cols_in, bands):
    vmem, hbm = pl.BlockSpec(memory_space=pltpu.VMEM), pl.BlockSpec(memory_space=pltpu.HBM)
    into, back = permutations()
    eye = jnp.asarray(np.eye(128), BF16)
    enter, encode, coarse, deeper, decode, output, merge, biases = bands
    operands = (sky, dirty_in, rows_in, cols_in, eye, into, enter, biases)
    operands += (encode, coarse, deeper, merge, decode, output, back)
    return pl.pallas_call(
        network_kernel,
        out_shape=(
            jax.ShapeDtypeStruct((128, 256), F32),
            jax.ShapeDtypeStruct((128, 256), F32),
        ),
        in_specs=[hbm] * len(operands),
        out_specs=(hbm, vmem),
        scratch_shapes=[pltpu.VMEM(x.shape, x.dtype) for x in operands]
        + [
            pltpu.VMEM((2, 192, 384), BF16),
            pltpu.VMEM((5, 20, 16, 128), BF16),
            pltpu.VMEM((38, 20, 16, 128), BF16),
            pltpu.VMEM((38, 20, 16, 128), BF16),
            pltpu.VMEM((38, 20, 16, 128), BF16),
            pltpu.VMEM((38, 11, 16, 128), BF16),
            pltpu.VMEM((38, 11, 16, 128), BF16),
            pltpu.VMEM((36, 9, 16, 128), BF16),
            pltpu.VMEM((20, 16, 128), F32),
            pltpu.VMEM((2, 320, 256), F32),
            pltpu.VMEM((128, 256), F32),
            pltpu.SemaphoreType.DMA((len(operands) + 1,)),
        ],
        compiler_params=pltpu.CompilerParams(vmem_limit_bytes=64 << 20),
        name="network",
    )(*operands)


def raw_weights(ew, eb, nw, nb, cw, cb, dw, db, uw, sw, mb, ow, ob, fw):
    biases = tuple(b.reshape(1, -1) for b in (eb, nb, cb, db, mb, ob))
    return (
        jnp.swapaxes(ew, 2, 3),
        nw,
        jnp.swapaxes(cw, 2, 3),
        dw,
        ow,
        fw[:, :, 0, :],
        uw,
        sw,
    ) + biases


def shards(
    sky_image,
    visibilities,
    grid_kernels,
    tile_counts,
    block_tiles,
    *parameters,
):
    slots = block_tiles.shape[2]
    dirty, rows, cols, *bands = exchange(
        visibilities[0, 0],
        tile_counts.reshape(1, -1),
        block_tiles.reshape(1, -1),
        grid_kernels.reshape(slots * 64, 256),
        sky_image,
        raw_weights(*parameters),
    )
    return network(sky_image, dirty, rows, cols, tuple(bands))


def solution(mesh):
    block = P("gx", "gy")
    return jax.shard_map(
        shards,
        mesh=mesh,
        in_specs=(
            block,
            P("gx", "gy", None, None, None),
            P("gx", "gy", None, None, None),
            P("gx", "gy", None),
            P("gx", "gy", None),
        )
        + (P(),) * 14,
        out_specs=(block, block),
        check_vma=False,
    )
```

```python
import functools
import math

import jax
import jax.numpy as jnp
import numpy as np
from jax import lax
from jax.experimental import pallas as pl
from jax.experimental.pallas import tpu as pltpu
from jax.sharding import PartitionSpec as P

MESH = pl.DeviceIdType.MESH
F32 = jnp.float32
BF16 = jnp.bfloat16

GE, GC, GM, GN, GD = 9, 18, 9, 9, 9
NX, NY = 32, 16
SLABS = 18
STRIPES = 16
PIX = SLABS * STRIPES
PIX2 = PIX // 2
GROUPS = 18


def dot(a, b):
    return jnp.dot(a, b, preferred_element_type=F32)


def dot_nt(a, b):
    return lax.dot_general(a, b, (((1,), (1,)), ((), ())), preferred_element_type=F32)


def complex_block(c, s):
    return np.stack([np.stack([c, -s]), np.stack([s, c])])


def transform_constants():
    turn = 2.0 * math.pi
    y0 = np.arange(128)
    cells = np.arange(256)
    ang = turn * (np.outer(y0, y0) % 128) / 128
    first = complex_block(np.cos(ang), np.sin(ang))
    first = first.reshape(2, 2, 128, 16, 8).transpose(0, 2, 3, 1, 4).reshape(256, 256)
    ang = turn * np.outer(y0, cells % 32) / 4096
    sign = np.where(y0 % 2 == 0, 1.0, -1.0)[:, None]
    twist1 = np.stack([np.cos(ang) * sign, np.sin(ang) * sign])
    short = np.arange(32)
    ang = turn * (np.outer(short, short) % 32) / 32
    c32, s32 = np.cos(ang), np.sin(ang)
    second = complex_block(c32, s32)
    second = np.einsum("abys,rt->yarbts", second, np.eye(8)).reshape(512, 512)
    third = complex_block(c32, s32)
    third = np.einsum("abxi,yz->ayxibz", third, np.eye(8)).reshape(512, 512)
    ang = turn * np.outer(y0, y0) / 4096
    twist2 = np.stack([np.cos(ang) * sign, np.sin(ang) * sign]) / 4096
    ang = turn * (np.outer(short, y0) % 32) / 32
    fourth = np.concatenate([np.cos(ang), -np.sin(ang)], axis=1)
    return (
        jnp.asarray(first, BF16),
        jnp.asarray(twist1, F32),
        jnp.asarray(second, BF16),
        jnp.asarray(third, BF16),
        jnp.asarray(twist2, F32),
        jnp.asarray(fourth, BF16),
        jnp.asarray(np.eye(128), BF16),
    )


def permutations():
    into = np.zeros((20, STRIPES, 384), np.float32)
    back = np.zeros((256, SLABS, STRIPES), np.float32)
    for w in range(-1, SLABS + 1):
        for s in range(STRIPES):
            col = SLABS * s + w - 8
            if 0 <= col < 264:
                into[w + 1, s, col] = 1
            elif -8 <= col < 0:
                into[w + 1, s, 384 + col] = 1
            if 0 <= col < 256 and 0 <= w < SLABS:
                back[col, w, s] = 1
    return jnp.asarray(into.reshape(320, 384), BF16), jnp.asarray(back.reshape(256, PIX), BF16)


def farthest_first(step, count, me):
    away = (step + 1) // 2
    shift = count // 2 + jnp.where(step % 2 == 1, away, -away)
    return lax.rem(me + shift, count)


def send_all(axis, count, me, source, landing, send_sem, recv_sem):
    def one(step, carry):
        other = farthest_first(step, count, me)
        pltpu.make_async_remote_copy(
            src_ref=source.at[other],
            dst_ref=landing.at[me],
            send_sem=send_sem,
            recv_sem=recv_sem,
            device_id={axis: other},
            device_id_type=MESH,
        ).start()
        return carry

    lax.fori_loop(0, count - 1, one, 0)
    landing[me] = source[me]


def wait_bytes(ref, sem):
    pltpu.make_async_copy(ref, ref, sem).wait()


def grid_tiles(vis, counts, owner, kernels):
    wide = vis[...].astype(F32)
    parts = [jnp.concatenate([wide[:, k, :]] * 2, axis=1) for k in range(2)]
    slot = lax.broadcasted_iota(jnp.int32, (64, 128), 0)
    half = lax.broadcasted_iota(jnp.int32, (64, 128), 1) // 64
    contrib = None
    for piece in range(8):
        blocks = []
        for q in range(4 * piece, 4 * piece + 4):
            hit = slot == 2 * q + half
            block = [jnp.where(hit, part, 0.0).astype(BF16) for part in parts]
            blocks.append(jnp.concatenate(block, axis=0))
        term = dot(jnp.concatenate(blocks, axis=1), kernels[512 * piece : 512 * piece + 512, :])
        contrib = term if contrib is None else contrib + term
    live = jnp.sum(counts[...], axis=1, keepdims=True)
    both = jnp.concatenate([owner[...]] * 2, axis=1)
    lane = lax.broadcasted_iota(jnp.int32, (1, 128), 1) % 64
    both = jnp.where(lane < live, both, -1)
    chosen = jnp.where(lax.broadcasted_iota(jnp.int32, (128, 128), 0) == both, 1.0, 0.0)
    chosen = chosen.astype(BF16)
    sums = []
    for k in range(2):
        own = contrib[64 * k : 64 * k + 64]
        high = own.astype(BF16)
        low = (own - high.astype(F32)).astype(BF16)
        total = dot(chosen, jnp.concatenate([high, low], axis=0))
        sums.append(total.reshape(16, 8, 256))
    return jnp.concatenate(sums, axis=1).astype(BF16)


def column_transform(held, first, twist1, second):
    turned = dot(first[...], held)
    real, imag = turned[:128], turned[128:]
    c, s = twist1[0], twist1[1]
    both = jnp.concatenate([real * c - imag * s, real * s + imag * c], axis=1).astype(BF16)
    return dot_nt(second[...], both)


def columns_up(held, eye):
    wide = held.astype(F32).reshape(16, 4, 8, 128)
    halves = []
    for y1 in range(2):
        parts = []
        for part in range(2):
            piece = wide[:, 2 * y1 + part].reshape(128, 128).astype(BF16)
            parts.append(dot_nt(eye, piece).reshape(16, 8, 128))
        halves.append(jnp.concatenate(parts, axis=1))
    return jnp.concatenate(halves, axis=0).astype(BF16)


def row_transform(held, third, twist2, fourth, store):
    turned = dot(third[...], held)
    for y in range(8):
        real = turned[32 * y : 32 * y + 32]
        imag = turned[256 + 32 * y : 256 + 32 * y + 32]
        real = jnp.concatenate([real] * 4, axis=0)
        imag = jnp.concatenate([imag] * 4, axis=0)
        c, s = twist2[0], twist2[1]
        both = jnp.concatenate([real * c - imag * s, real * s + imag * c], axis=1).astype(BF16)
        store(y, dot_nt(fourth[...], both))


def repeat_matrix(rows):
    row = lax.broadcasted_iota(jnp.int32, (rows, 256), 0)
    lane = lax.broadcasted_iota(jnp.int32, (rows, 256), 1)
    return jnp.where(lane % rows == row, 1.0, 0.0).astype(BF16)


def dot_tn(a, b):
    return lax.dot_general(a, b, (((0,), (0,)), ((), ())), preferred_element_type=F32)


def band(dst, tile, high, rows, out_row, place, lane_id, count):
    for dc in range(3):
        taps = [tile(p, dc) for p in range(3)]
        for row in rows:
            block = jnp.zeros(lane_id.shape, F32)
            for p in range(3):
                if 0 <= out_row(row, p) < count:
                    block = block + jnp.where(lane_id == out_row(row, p), taps[p], 0.0)
            at = place(dc, row)
            dst[at : at + high, :] = block.astype(BF16)


def place_fine(dc, row):
    if row == 3:
        return (800, 864, 992)[dc]
    if row == 12:
        return (832, 768, 896)[dc]
    return 256 * dc + 32 * (row - 4)


def place_coarse(dc, row):
    if row < 4:
        return 768 + 128 * dc + 64 + 32 * (row - 2)
    if row > 11:
        return 768 + 128 * dc + 32 * (row - 12)
    return 256 * dc + 32 * (row - 4)


def place_deeper(dc, row):
    if row == 1:
        return 768 + 128 * dc + 64
    if row == 6:
        return 768 + 128 * dc
    return 256 * dc + 64 * (row - 2)


def exchange_kernel(*refs):
    (
        first_h,
        twist1_h,
        second_h,
        third_h,
        twist2_h,
        fourth_h,
        eye_h,
        kernels_h,
        vis_h,
        counts_h,
        owner_h,
        sky_h,
    ) = refs[:12]
    weights_h = refs[12:26]
    dirty_out, rows_out, cols_out = refs[26:29]
    bands_out = refs[29:37]
    (
        first,
        twist1,
        second,
        third,
        twist2,
        fourth,
        eye,
        kernels,
        vis,
        counts,
        owner,
        sky,
    ) = refs[37:49]
    weights = refs[49:63]
    built = refs[63:71]
    w_enter, w_encode, w_coarse, w_deeper, w_decode, w_output, w_merge, biases = built
    (
        tiles,
        landed1,
        bands,
        landed2,
        ups,
        landed3,
        image,
        downs,
        landed4,
        sides,
        sky_rows,
        sky_sides,
        sky_cols,
        sky_own,
        send_sem,
        recv_sem,
        load_sem,
        save_sem,
    ) = refs[71:]
    saves = [
        pltpu.make_async_copy(source, target, save_sem.at[k])
        for k, (source, target) in enumerate(zip(built, bands_out))
    ]
    save_rows = pltpu.make_async_copy(sky_rows, rows_out, save_sem.at[8])
    save_cols = pltpu.make_async_copy(sky_sides, cols_out, save_sem.at[9])
    save_main = pltpu.make_async_copy(landed4, dirty_out.at[pl.ds(0, 32)], save_sem.at[10])
    save_sides = pltpu.make_async_copy(sides, dirty_out.at[pl.ds(32, 2)], save_sem.at[11])
    gx, gy = lax.axis_index("gx"), lax.axis_index("gy")
    down_x, up_x = lax.rem(gx + 1, NX), lax.rem(gx + NX - 1, NX)
    right_y, left_y = lax.rem(gy + 1, NY), lax.rem(gy + NY - 1, NY)
    barrier = pltpu.get_barrier_semaphore()

    def greet(axis, count, me):
        def one(step, carry):
            other = farthest_first(step, count, me)
            pl.semaphore_signal(barrier, inc=1, device_id={axis: other}, device_id_type=MESH)
            return carry

        lax.fori_loop(0, count - 1, one, 0)

    greet("gy", NY, gy)
    greet("gx", NX, gx)
    for x, y in ((NX - 1, left_y), (0, right_y)):
        pl.semaphore_signal(barrier, inc=1, device_id={"gx": x, "gy": y}, device_id_type=MESH)

    sources = (kernels_h, vis_h, counts_h, owner_h, sky_h, first_h, twist1_h, second_h)
    sources += weights_h + (third_h, twist2_h, fourth_h, eye_h)
    targets = (kernels, vis, counts, owner, sky, first, twist1, second)
    targets += weights + (third, twist2, fourth, eye)
    loads = [
        pltpu.make_async_copy(source, target, load_sem.at[k])
        for k, (source, target) in enumerate(zip(sources, targets))
    ]
    for load in loads:
        load.start()

    for load in loads[:5]:
        load.wait()
    sky_own[...] = sky[...].astype(BF16)
    tiles[...] = grid_tiles(vis, counts, owner, kernels)
    edge = jnp.where((gx == 0) | (gx == NX - 1), NX, 0)
    pl.semaphore_wait(barrier, NX + NY - 2 + edge)

    send_all("gy", NY, gy, tiles, landed1, send_sem.at[0], recv_sem.at[0])

    def to_side(source, target, slot, axis, other):
        return pltpu.make_async_remote_copy(
            src_ref=source,
            dst_ref=target,
            send_sem=send_sem.at[slot],
            recv_sem=recv_sem.at[slot],
            device_id={axis: other},
            device_id_type=MESH,
        )

    row_copies = [
        to_side(sky_own.at[pl.ds(112, 16)], sky_rows.at[0], 4, "gx", down_x),
        to_side(sky_own.at[pl.ds(0, 16)], sky_rows.at[1], 5, "gx", up_x),
    ]
    for copy in row_copies:
        copy.start()

    for load in loads[5:]:
        load.wait()
    enter_w, encode_w, coarse_w, deeper_w, decode_w, output_w, upward_w, skip_w = weights[:8]
    rep32, rep64 = repeat_matrix(32), repeat_matrix(64)
    lane32 = lax.broadcasted_iota(jnp.int32, (32, 256), 1)
    lane64 = lax.broadcasted_iota(jnp.int32, (64, 256), 1)
    rows = range(3, 13)

    def fine_row(row, p):
        return row - 3 - p

    for dst, raw, save in ((w_encode, encode_w, saves[1]), (w_decode, decode_w, saves[4])):
        dst[928:992, :] = jnp.zeros((64, 256), BF16)

        def tile(p, dc, raw=raw):
            return dot_tn(raw[p, dc], rep32)

        band(dst, tile, 32, rows, fine_row, place_fine, lane32 // 32, 8)
        save.start()

    wait_bytes(landed1.at[pl.ds(0, 15)], recv_sem.at[0])
    turned = column_transform(landed1[...].reshape(256, 256), first, twist1, second)
    bands[...] = turned.astype(BF16).reshape(16, 32, 128)
    send_all("gy", NY, gy, bands, landed2, send_sem.at[1], recv_sem.at[1])

    for copy in row_copies:
        copy.wait()
    above, below = sky_rows[0].astype(F32)[8:16], sky_rows[1].astype(F32)[0:8]
    outer_rows = jnp.concatenate([below, jnp.zeros((112, 256), F32), above], axis=0).astype(BF16)
    for half, chosen, at in ((0, eye[0:16], 0), (1, eye[112:128], 8)):
        lanes = slice(128 * half, 128 * half + 128)
        both = [dot_nt(chosen, sky_own[:, lanes]), dot_nt(chosen, outer_rows[:, lanes])]
        both = [part[at : at + 8] for part in both]
        sky_cols[half] = jnp.concatenate(both, axis=0).astype(BF16)
    col_copies = [
        to_side(sky_cols.at[1], sky_sides.at[0], 6, "gy", right_y),
        to_side(sky_cols.at[0], sky_sides.at[1], 7, "gy", left_y),
    ]
    for copy in col_copies:
        copy.start()

    def coarse_tile(p, dc):
        return dot(coarse_w[p, dc], rep64)

    def coarse_row(row, p):
        return row // 2 - 1 - p

    band(w_coarse, coarse_tile, 32, range(2, 14), coarse_row, place_coarse, lane32 // 64, 4)
    saves[2].start()

    def deeper_tile(p, dc):
        return dot_tn(deeper_w[p, dc], rep64)

    def deeper_row(row, p):
        return row - 1 - p

    band(w_deeper, deeper_tile, 64, range(1, 7), deeper_row, place_deeper, lane64 // 64, 4)
    saves[3].start()
    tap_row = lax.broadcasted_iota(jnp.int32, (3, 256), 0)
    tap_lane = lax.broadcasted_iota(jnp.int32, (3, 256), 1) // 64
    own = jnp.where(tap_row == tap_lane, 1.0, 0.0).astype(BF16)
    taps = [dot_tn(output_w[p], own) for p in range(3)]
    for row in range(16):
        block = jnp.zeros((32, 256), F32)
        for p in range(3):
            if 0 <= row - 3 - p < 8:
                block = block + jnp.where(lane32 % 8 == row - 3 - p, taps[p], 0.0)
        w_output[32 * row : 32 * row + 32, :] = block.astype(BF16)
    saves[5].start()

    wait_bytes(landed2.at[pl.ds(0, 15)], recv_sem.at[1])
    ups[...] = columns_up(landed2[...], eye[...])
    send_all("gx", NX, gx, ups, landed3, send_sem.at[2], recv_sem.at[2])

    lifted = dot_tn(upward_w[...], rep32)
    for row in range(4):
        block = jnp.where(lane64 // 64 == row, lifted, 0.0)
        w_merge[256 + 64 * row : 320 + 64 * row, :] = block.astype(BF16)
    skipped = dot_tn(skip_w[...], rep32)
    for row in range(8):
        block = jnp.where(lane32 // 32 == row, skipped, 0.0)
        w_merge[32 * row : 32 * row + 32, :] = block.astype(BF16)
    row_id = lax.broadcasted_iota(jnp.int32, (64, 256), 0)
    for dc in range(3):
        taps = [dot(enter_w[p, dc], rep32) for p in range(3)]
        for variant in range(4):
            for channel in range(2):
                block = jnp.zeros((64, 256), F32)
                for p in range(3):
                    hit = row_id - 15 - 8 * variant - p == lane64 // 32
                    block = block + jnp.where(hit, taps[p][channel : channel + 1, :], 0.0)
                at = dc * 128 + channel * 64
                w_enter[variant, at : at + 64, :] = block.astype(BF16)
    for row, ref in enumerate(weights[8:]):
        biases[row : row + 1, :] = jnp.concatenate([ref[...]] * (256 // ref.shape[1]), axis=1)
    biases[6:8, :] = jnp.zeros((2, 256), F32)
    for k in (0, 6, 7):
        saves[k].start()

    def store(y, value):
        image[pl.ds(8 + y, 32, stride=8), :] = value

    image[0:8] = jnp.zeros((8, 128), F32)
    image[264:272] = jnp.zeros((8, 128), F32)

    wait_bytes(landed3.at[pl.ds(0, 31)], recv_sem.at[2])
    row_transform(landed3[...].reshape(512, 128), third, twist2, fourth, store)
    whole = image[...].reshape(34, 8, 128)
    lane = lax.broadcasted_iota(jnp.int32, (32, 8, 128), 2)
    outer = jnp.where(lane < 64, whole[2:34], whole[0:32])
    downs[...] = jnp.concatenate([whole[1:33], outer], axis=1).astype(BF16)
    send_all("gx", NX, gx, downs, landed4, send_sem.at[3], recv_sem.at[3])

    def beside(other_y, slot):
        def one(x, carry):
            pltpu.make_async_remote_copy(
                src_ref=downs.at[x],
                dst_ref=sides.at[slot],
                send_sem=send_sem.at[8 + slot],
                recv_sem=recv_sem.at[8 + slot],
                device_id={"gx": x, "gy": other_y},
                device_id_type=MESH,
            ).start()
            return carry

        lax.fori_loop(0, NX, one, 0)

    @pl.when(gx == NX - 1)
    def _():
        beside(right_y, 0)

    @pl.when(gx == 0)
    def _():
        beside(left_y, 1)

    for copy in col_copies:
        copy.wait()
    save_rows.start()
    save_cols.start()

    wait_bytes(landed4.at[pl.ds(0, 31)], recv_sem.at[3])
    save_main.start()
    wait_bytes(sides.at[0], recv_sem.at[8])
    wait_bytes(sides.at[1], recv_sem.at[9])
    save_sides.start()
    for save in saves + [save_rows, save_cols]:
        save.wait()
    save_main.wait()
    save_sides.wait()
    wait_bytes(tiles.at[pl.ds(0, 15)], send_sem.at[0])
    wait_bytes(bands.at[pl.ds(0, 15)], send_sem.at[1])
    wait_bytes(ups.at[pl.ds(0, 31)], send_sem.at[2])
    wait_bytes(downs.at[pl.ds(0, 31)], send_sem.at[3])

    @pl.when(gx == NX - 1)
    def _():
        wait_bytes(downs, send_sem.at[8])

    @pl.when(gx == 0)
    def _():
        wait_bytes(downs, send_sem.at[9])


def exchange(vis, counts, owner, kernels, sky, weights):
    hbm = pl.BlockSpec(memory_space=pltpu.HBM)
    operands = transform_constants() + (kernels, vis, counts, owner, sky) + weights
    shapes = [
        (34, 16, 128),
        (2, 16, 256),
        (2, 16, 128),
        (4, 384, 256),
        (1024, 256),
        (1152, 256),
        (1152, 256),
        (1024, 256),
        (512, 256),
        (512, 256),
    ]
    outs = [jax.ShapeDtypeStruct(shape, BF16) for shape in shapes]
    outs.append(jax.ShapeDtypeStruct((8, 256), F32))
    return pl.pallas_call(
        exchange_kernel,
        out_shape=tuple(outs),
        in_specs=[hbm] * len(operands),
        out_specs=(hbm,) * len(outs),
        scratch_shapes=[pltpu.VMEM(x.shape, x.dtype) for x in list(operands) + outs[3:]]
        + [
            pltpu.VMEM((16, 16, 256), BF16),
            pltpu.VMEM((16, 16, 256), BF16),
            pltpu.VMEM((16, 32, 128), BF16),
            pltpu.VMEM((16, 32, 128), BF16),
            pltpu.VMEM((32, 16, 128), BF16),
            pltpu.VMEM((32, 16, 128), BF16),
            pltpu.VMEM((272, 128), F32),
            pltpu.VMEM((32, 16, 128), BF16),
            pltpu.VMEM((32, 16, 128), BF16),
            pltpu.VMEM((2, 16, 128), BF16),
            pltpu.VMEM((2, 16, 256), BF16),
            pltpu.VMEM((2, 16, 128), BF16),
            pltpu.VMEM((2, 16, 128), BF16),
            pltpu.VMEM((128, 256), BF16),
            pltpu.SemaphoreType.DMA((10,)),
            pltpu.SemaphoreType.DMA((10,)),
            pltpu.SemaphoreType.DMA((len(operands),)),
            pltpu.SemaphoreType.DMA((12,)),
        ],
        compiler_params=pltpu.CompilerParams(
            collective_id=0, has_side_effects=True, vmem_limit_bytes=64 << 20
        ),
        name="exchange",
    )(*operands)


def network_kernel(*refs):
    sources, (dirty_hbm, estimate_out), targets = refs[:15], refs[15:17], refs[17:32]
    window, entry, fine_a, fine_b, fine_c, pooled, coarse, deep, mask, drawn, dirty_out, load_sem = refs[32:]
    save_dirty = pltpu.make_async_copy(dirty_out, dirty_hbm, load_sem.at[15])
    loads = [
        pltpu.make_async_copy(source, target, load_sem.at[k])
        for k, (source, target) in enumerate(zip(sources, targets))
    ]
    for load in loads:
        load.start()
    sky, dirty_in, rows_in, cols_in, eye, into, w_enter, biases = targets[:8]
    w_encode, w_coarse, w_deeper, w_merge, w_decode, w_output, back = targets[8:]

    def arrived(first, last):
        for load in loads[first:last]:
            load.wait()

    gx, gy = lax.axis_index("gx"), lax.axis_index("gy")
    last_x, last_y = lax.axis_size("gx") - 1, lax.axis_size("gy") - 1
    keep_top = jnp.where(gx == 0, 0.0, 1.0).astype(F32)
    keep_bottom = jnp.where(gx == last_x, 0.0, 1.0).astype(F32)

    slab = lax.broadcasted_iota(jnp.int32, (20, 16, 128), 0)
    stripe = lax.broadcasted_iota(jnp.int32, (20, 16, 128), 1)
    col = SLABS * stripe + slab - 9 + 256 * gy
    mask[...] = jnp.where((col >= 0) & (col < 256 * (last_y + 1)), 1.0, 0.0).astype(F32)

    blank = jnp.zeros((20, 16, 128), BF16)
    for ref, top in ((fine_a, 37), (fine_b, 37), (fine_c, 37), (pooled, 37), (coarse, 37)):
        ref[0] = blank[: ref.shape[1]]
        ref[top] = blank[: ref.shape[1]]

    arrived(0, 6)
    above = rows_in[0].astype(F32)[8:16] * keep_top
    below = rows_in[1].astype(F32)[0:8] * keep_bottom
    zeros = jnp.zeros((32, 512), F32)
    window[0, :, 0:256] = jnp.concatenate(
        [zeros[:16, :256], above, sky[...], below, zeros[:, :256]], axis=0
    ).astype(BF16)
    wide, sides = dirty_in[...].astype(F32), cols_in[...].astype(F32)
    gap = jnp.zeros((112, 128), F32)
    parts = []
    for half in range(2):
        rows8 = slice(8 * half, 8 * half + 8)
        stacked = [wide[0:32, rows8].reshape(256, 128), wide[33, rows8], gap, wide[32, rows8]]
        stacked += [sides[1, rows8], gap, sides[0, rows8]]
        parts.append(dot_nt(eye[...], jnp.concatenate(stacked, axis=0).astype(BF16)))
    dirty_out[...] = parts[0][:, 0:256]
    save_dirty.start()
    whole = jnp.concatenate(
        [zeros[:16], parts[1][120:128] * keep_top, parts[0], parts[1][0:8] * keep_bottom, zeros],
        axis=0,
    ).astype(BF16)
    window[1] = whole[:, 0:384]
    window[0, :, 256:384] = whole[:, 384:512]
    pieces = []
    for q in range(5):
        rows64 = slice(32 * q, 32 * q + 64)
        pieces += [window[0, rows64], window[1, rows64]]
    placed = dot_nt(into[...], jnp.concatenate(pieces, axis=0))
    for q in range(5):
        value = placed[:, 128 * q : 128 * q + 128].reshape(20, 16, 128) * mask[...]
        entry[q] = value.astype(BF16)

    def row_keep(group):
        top = jnp.where(group == 0, keep_top, 1.0)
        bottom = jnp.where(group == GROUPS - 1, keep_bottom, 1.0)
        return top * bottom

    def put(ref, at, value, slabs):
        ref[at, 1 : slabs + 1] = value.astype(BF16)
        ref[at, 0] = pltpu.roll(value[slabs - 1], 1, 0).astype(BF16)
        ref[at, slabs + 1] = pltpu.roll(value[0], STRIPES - 1, 0).astype(BF16)

    def finish(total, bias_row, keep):
        value = jnp.maximum(total + biases[bias_row : bias_row + 1, :], 0.0)
        scaled = mask[1:19] if keep is None else mask[1:19] * keep
        return [
            value[:, 128 * h : 128 * h + 128].reshape(SLABS, 16, 128) * scaled for h in range(2)
        ]

    def beside(ref, group, slabs):
        lanes = lax.broadcasted_iota(jnp.int32, (slabs, 16, 128), 2)
        return jnp.where(lanes < 64, ref[2 * group + 3, 0:slabs], ref[2 * group, 0:slabs])

    def gathered(ref, first, count, slabs, pack):
        columns = [[] for _ in range(8 if pack else 9)]
        for group in range(count):
            group = first + group
            for dc in range(3):
                for h in range(2):
                    piece = ref[2 * group + 1 + h, dc : dc + slabs]
                    columns[2 * dc + h].append(piece.reshape(slabs * 16, 128))
            edge = beside(ref, group, slabs + 2)
            edges = [edge[dc : dc + slabs].reshape(slabs * 16, 128) for dc in range(3)]
            if pack:
                lanes = lax.broadcasted_iota(jnp.int32, (slabs * 16, 128), 1)
                turned = jnp.concatenate([edges[0][:, 64:], edges[0][:, :64]], axis=1)
                middle = (lanes >= 32) & (lanes < 96)
                edges = [jnp.where(middle, turned, edges[1]), edges[2]]
            for k, edge in enumerate(edges):
                columns[6 + k].append(edge)
        return jnp.concatenate([jnp.concatenate(c, axis=0) for c in columns], axis=1)

    arrived(6, 8)
    for variant in range(4):
        members = list(range(variant, GROUPS, 4))
        pieces = []
        for dc in range(3):
            rows = [entry[group // 4, dc : dc + SLABS].reshape(PIX, 128) for group in members]
            pieces.append(jnp.concatenate(rows, axis=0))
        total = dot(jnp.concatenate(pieces, axis=1), w_enter[variant])
        for g, group in enumerate(members):
            keep = row_keep(group) if group in (0, GROUPS - 1) else None
            for h, value in enumerate(finish(total[PIX * g : PIX * g + PIX], 0, keep)):
                put(fine_a, 2 * group + 1 + h, value, SLABS)

    def encode_step(step, carry):
        total = dot(gathered(fine_a, GE * step, GE, SLABS, True), w_encode[...])
        for g in range(GE):
            group = GE * step + g
            keep = row_keep(group) if g in (0, GE - 1) else None
            for h, value in enumerate(finish(total[PIX * g : PIX * g + PIX], 1, keep)):
                put(fine_b, 2 * group + 1 + h, value, SLABS)
                pair = value.reshape(SLABS // 2, 2, 16, 128)
                put(pooled, 2 * group + 1 + h, (pair[:, 0] + pair[:, 1]) * 0.25, SLABS // 2)
        return carry

    arrived(8, 9)
    lax.fori_loop(0, GROUPS // GE, encode_step, 0)

    even_mask = mask[1:19].reshape(SLABS // 2, 2, 16, 128)[:, 0]

    def coarse_step(step, carry):
        total = dot(gathered(pooled, GC * step, GC, SLABS // 2, False), w_coarse[...])
        for g in range(GC):
            group = GC * step + g
            value = jnp.maximum(total[PIX2 * g : PIX2 * g + PIX2] + biases[2:3, :], 0.0)
            scaled = even_mask * row_keep(group) if g in (0, GC - 1) else even_mask
            for h in range(2):
                half = value[:, 128 * h : 128 * h + 128].reshape(SLABS // 2, 16, 128) * scaled
                put(coarse, 2 * group + 1 + h, half, SLABS // 2)
        return carry

    arrived(9, 10)
    lax.fori_loop(0, GROUPS // GC, coarse_step, 0)

    def deeper_step(step, carry):
        total = dot(gathered(coarse, GM * step, GM, SLABS // 2, False), w_deeper[...])
        value = jnp.maximum(total + biases[3:4, :], 0.0).astype(BF16)
        for g in range(GM):
            piece = value[PIX2 * g : PIX2 * g + PIX2].reshape(SLABS // 2, 16, 256)
            for h in range(2):
                deep[2 * (GM * step + g) + h] = piece[:, :, 128 * h : 128 * h + 128]
        return carry

    arrived(10, 11)
    lax.fori_loop(0, GROUPS // GM, deeper_step, 0)

    def merge_step(step, carry):
        columns = []
        for h in range(2):
            rows = [
                fine_b[2 * (GN * step + g) + 1 + h, 1:19].reshape(PIX, 128) for g in range(GN)
            ]
            columns.append(jnp.concatenate(rows, axis=0))
        for h in range(2):
            rows = []
            for g in range(GN):
                low = deep[2 * (GN * step + g) + h].reshape(SLABS // 2, 1, 16, 128)
                low = jnp.broadcast_to(low, (SLABS // 2, 2, 16, 128))
                rows.append(low.reshape(PIX, 128))
            columns.append(jnp.concatenate(rows, axis=0))
        total = dot(jnp.concatenate(columns, axis=1), w_merge[...])
        for g in range(GN):
            group = GN * step + g
            keep = row_keep(group) if g in (0, GN - 1) else None
            for h, half in enumerate(finish(total[PIX * g : PIX * g + PIX], 4, keep)):
                put(fine_a, 2 * group + 1 + h, half, SLABS)
        return carry

    arrived(11, 12)
    lax.fori_loop(0, GROUPS // GN, merge_step, 0)

    def decode_step(step, carry):
        total = dot(gathered(fine_a, GD * step, GD, SLABS, True), w_decode[...])
        for g in range(GD):
            group = GD * step + g
            keep = row_keep(group) if g in (0, GD - 1) else None
            for h, half in enumerate(finish(total[PIX * g : PIX * g + PIX], 5, keep)):
                put(fine_c, 2 * group + 1 + h, half, SLABS)
        return carry

    arrived(12, 13)
    lax.fori_loop(0, GROUPS // GD, decode_step, 0)

    lane_row = lax.broadcasted_iota(jnp.int32, (320, 256), 1) // 8 % 8

    def output_step(half, carry):
        columns = []
        for h in range(4):
            rows = [fine_c[2 * (8 * half + g + 1) + h].reshape(320, 128) for g in range(8)]
            columns.append(jnp.concatenate(rows, axis=0))
        total = dot(jnp.concatenate(columns, axis=1), w_output[...])
        kept = total[0:320]
        for g in range(1, 8):
            kept = jnp.where(lane_row == g, total[320 * g : 320 * g + 320], kept)
        drawn[half] = kept
        return carry

    arrived(13, 15)
    lax.fori_loop(0, 2, output_step, 0)

    sums = []
    for half in range(2):
        taps = drawn[half].reshape(20, 16, 256)
        left = taps[0:18, :, 0:128] + taps[2:20, :, 128:256]
        middle = taps[1:19, :, 0:128].reshape(PIX, 128)
        sums.append((left.reshape(PIX, 128), pltpu.roll(middle, 64, 1)))
    lanes = lax.broadcasted_iota(jnp.int32, (PIX, 128), 1)
    upper = sums[0][0] + sums[0][1]
    lower = pltpu.roll(sums[1][0] + sums[1][1], 64, 1)
    update = jnp.where(lanes < 64, upper, lower)
    high = update.astype(BF16)
    low = (update - high.astype(F32)).astype(BF16)
    ordered = dot(back[...], high) + dot(back[...], low)
    estimate_out[...] = sky[...] + ordered.T
    save_dirty.wait()


def network(sky, dirty_in, rows_in, cols_in, bands):
    vmem, hbm = pl.BlockSpec(memory_space=pltpu.VMEM), pl.BlockSpec(memory_space=pltpu.HBM)
    into, back = permutations()
    eye = jnp.asarray(np.eye(128), BF16)
    enter, encode, coarse, deeper, decode, output, merge, biases = bands
    operands = (sky, dirty_in, rows_in, cols_in, eye, into, enter, biases)
    operands += (encode, coarse, deeper, merge, decode, output, back)
    return pl.pallas_call(
        network_kernel,
        out_shape=(
            jax.ShapeDtypeStruct((128, 256), F32),
            jax.ShapeDtypeStruct((128, 256), F32),
        ),
        in_specs=[hbm] * len(operands),
        out_specs=(hbm, vmem),
        scratch_shapes=[pltpu.VMEM(x.shape, x.dtype) for x in operands]
        + [
            pltpu.VMEM((2, 192, 384), BF16),
            pltpu.VMEM((5, 20, 16, 128), BF16),
            pltpu.VMEM((38, 20, 16, 128), BF16),
            pltpu.VMEM((38, 20, 16, 128), BF16),
            pltpu.VMEM((38, 20, 16, 128), BF16),
            pltpu.VMEM((38, 11, 16, 128), BF16),
            pltpu.VMEM((38, 11, 16, 128), BF16),
            pltpu.VMEM((36, 9, 16, 128), BF16),
            pltpu.VMEM((20, 16, 128), F32),
            pltpu.VMEM((2, 320, 256), F32),
            pltpu.VMEM((128, 256), F32),
            pltpu.SemaphoreType.DMA((len(operands) + 1,)),
        ],
        compiler_params=pltpu.CompilerParams(vmem_limit_bytes=64 << 20),
        name="network",
    )(*operands)


def raw_weights(ew, eb, nw, nb, cw, cb, dw, db, uw, sw, mb, ow, ob, fw):
    biases = tuple(b.reshape(1, -1) for b in (eb, nb, cb, db, mb, ob))
    return (
        jnp.swapaxes(ew, 2, 3),
        nw,
        jnp.swapaxes(cw, 2, 3),
        dw,
        ow,
        fw[:, :, 0, :],
        uw,
        sw,
    ) + biases


def shards(
    sky_image,
    visibilities,
    grid_kernels,
    tile_counts,
    block_tiles,
    *parameters,
):
    slots = block_tiles.shape[2]
    dirty, rows, cols, *bands = exchange(
        visibilities[0, 0],
        tile_counts.reshape(1, -1),
        block_tiles.reshape(1, -1),
        grid_kernels.reshape(slots * 64, 256),
        sky_image,
        raw_weights(*parameters),
    )
    return network(sky_image, dirty, rows, cols, tuple(bands))


def solution(mesh):
    block = P("gx", "gy")
    return jax.shard_map(
        shards,
        mesh=mesh,
        in_specs=(
            block,
            P("gx", "gy", None, None, None),
            P("gx", "gy", None, None, None),
            P("gx", "gy", None),
            P("gx", "gy", None),
        )
        + (P(),) * 14,
        out_specs=(block, block),
        check_vma=False,
    )
```
